256 devices in a mesh: vox: 32 (over x, y, core), row: 8 (over z).
Axes of the slice: x: 4, y: 4, z: 8, core: 2. Of those that a mesh axis runs over, the one named last changes fastest.
Arguments:
- tile_values: float32 [32768, 128, 128], P(('vox', 'row')), may hold values from -0.375 to 0.375
- tile_vox: int32 [32768], P(('vox', 'row')), may hold values from 0 to 255
- tile_slot: int32 [32768], P(('vox', 'row')), may hold values from 0 to 127, as said below
- slot_block: int32 [256, 128], P(('vox', 'row')), may hold values from 0 to 64, as said below
- ray_data: float32 [16384, 128], P(('vox', 'row')), may hold values from -23 to 23
Outputs:
- solution: float32 [8192, 128], P('vox')
- ray_residual: float32 [16384, 128], P(('vox', 'row'))
- normal_residual: float32 [8192, 128], P('vox')
The draws below stay inside these ranges and needn't reach their ends.
Inputs may be any that keep to these rules, and one draw needn't show every extreme that they name: `slot_block`: row g lists device g's send slots, 4 for each index d of vox in order. For each d the live slots come first and hold the index, 0 to 63, of one of the 64 ray blocks owned by the device at vox index d in g's row group; the other slots hold 64. Each device has at least one live slot for each d, and in every draw one index of vox receives 4 live slots from every device of its row group. `tile_slot`: every tile names a live slot of its own device, and every live slot of a device is named by at least one of its tiles.
All inputs are finite; a program needn't handle non-finite values.
Results may differ from the reference program's by a relative error of at most 0.0003.
Values sent between devices are 32-bit elements; how exact they have to be, the bound alone decides.
No kernel may reach another device: no remote copies, remote signals or barrier semaphores. Data moves between devices by JAX's collectives and lax.ppermute only.
A program may use at most 64 MiB of HBM per device.

```python
import jax
import jax.numpy as jnp
from jax import lax

TILE = 128
VT_DEV = 256
RB_DEV = 64
TILES_DEV = 128
CAP = 4
ITERS = 2
SLOTS = 128
RANKS = 256
ALL_TILES = 32768
VOXEL_TILES = 8192
RAY_BLOCKS = 16384
N_VOX = 32
N_ROW = 8


def shared_plan(key):
    key_count, key_hot, key_block, key_order, key_extra = jax.random.split(key, 5)
    counts = jax.random.randint(key_count, (RANKS, N_VOX), 1, CAP + 1)
    hottest = jax.random.randint(key_hot, (), 0, N_VOX)
    counts = jnp.where(jnp.arange(N_VOX)[None, :] == hottest, CAP, counts)
    live = (jnp.arange(CAP)[None, None, :] < counts[:, :, None]).reshape(RANKS, SLOTS)
    blocks = jax.random.randint(key_block, (RANKS, SLOTS), 0, RB_DEV)
    slot_table = jnp.where(live, blocks, RB_DEV).astype(jnp.int32)
    ordering = jnp.argsort(jnp.where(live, 0, 1).astype(jnp.int32), axis=1, stable=True).astype(jnp.int32)
    filled = jnp.sum(live.astype(jnp.int32), axis=1, keepdims=True)
    tile_order = jax.vmap(lambda sub: jax.random.permutation(sub, TILES_DEV))(jax.random.split(key_order, RANKS)).astype(jnp.int32)
    extra = jax.random.randint(key_extra, (RANKS, TILES_DEV), 0, filled)
    picked = jnp.where(tile_order < filled, tile_order, extra).astype(jnp.int32)
    slot_list = jnp.take_along_axis(ordering, picked, axis=1).reshape(RANKS * TILES_DEV)
    return (slot_table, slot_list.astype(jnp.int32))


def draw_slot_block(key, part):
    slot_table, slot_list = shared_plan(key)
    return slot_table


def draw_tile_slot(key, part):
    slot_table, slot_list = shared_plan(key)
    return slot_list


def draw_ray_data(key, part):
    key = jax.random.fold_in(key, 7)
    key_base, key_scale = jax.random.split(key)
    position = jnp.arange(RAY_BLOCKS, dtype=jnp.float32) / RAY_BLOCKS
    spread = jax.random.uniform(key_scale, (RAY_BLOCKS, 1), jnp.float32, -1.15, 1.15)
    row_scale = 0.6 * jnp.exp(spread) * jnp.power(3.0, position)[:, None]
    base = jax.random.truncated_normal(key_base, -4.0, 4.0, (RAY_BLOCKS, TILE), jnp.float32)
    return (base * row_scale).astype(jnp.float32)


def with_ends(array, key, least, largest):
    dims = array.shape
    index_at = [jax.random.randint(jax.random.fold_in(key, axis), (), 0, dims[axis]) for axis in range(len(dims))]
    array = array.at[tuple(index_at)].set(least)
    longest = dims.index(max(dims))
    index_at[longest] = (index_at[longest] + 1) % dims[longest]
    return array.at[tuple(index_at)].set(largest)


def steps_of(own_key, dims, cuts, least, top_value):
    loudness, own = 1.0, jax.random.fold_in(own_key, 6)
    for dim, shards_of in cuts:
        draws = jnp.exp(jax.random.uniform(jax.random.fold_in(own, dim), (shards_of,), jnp.float32, least / len(cuts), top_value / len(cuts)))
        loudness = loudness * jnp.repeat(draws, dims[dim] // shards_of).reshape([-1 if axis == dim else 1 for axis in range(len(dims))])
    return loudness


def normal_values(rng, dims, deviation, limit, pieces=(), kind=jnp.bfloat16):
    array = deviation * jax.random.normal(rng, dims, jnp.float32)
    if pieces:
        array = array * steps_of(rng, dims, pieces, -0.22, 0.18)
    return jnp.clip(array, -limit, limit).astype(kind)


def setup_inputs(seed: int = 0) -> dict:
    key_list = jax.random.split(jax.random.key(seed), 6)
    return {
        "tile_values": normal_values(key_list[0], (ALL_TILES, TILE, TILE), (2 * TILE) ** -0.5, 0.375, ((0, 256),), jnp.float32),
        "tile_vox": with_ends(jax.random.randint(key_list[1], (ALL_TILES,), 0, VT_DEV), jax.random.fold_in(key_list[1], 1), 0, VT_DEV - 1).astype(jnp.int32),
        "tile_slot": draw_tile_slot(jax.random.fold_in(key_list[5], 71), 0),
        "slot_block": draw_slot_block(jax.random.fold_in(key_list[5], 71), 0),
        "ray_data": draw_ray_data(jax.random.fold_in(key_list[5], 71), 0),
    }


def tile_maps(tile_vox, tile_slot, slot_block):
    ranks = jnp.arange(RANKS, dtype=jnp.int32)[:, None]
    vox_local = tile_vox.reshape(RANKS, TILES_DEV).astype(jnp.int32)
    slots = tile_slot.reshape(RANKS, TILES_DEV).astype(jnp.int32)
    local_block = jnp.take_along_axis(slot_block, slots, axis=1).astype(jnp.int32)
    voxel_index = (ranks // N_ROW) * VT_DEV + vox_local
    ray_index = ((slots // CAP) * N_ROW + ranks % N_ROW) * RB_DEV + local_block
    return voxel_index.astype(jnp.int32), ray_index.astype(jnp.int32)


def project(field, tiles, voxel_index, ray_index):
    def step(total, item):
        block, vox_rows, ray_rows = item
        part = jnp.einsum("tab,tb->ta", block, jnp.take(field, vox_rows, axis=0), precision=lax.Precision.HIGHEST)
        return total + jax.ops.segment_sum(part, ray_rows, num_segments=RAY_BLOCKS), None

    start = jnp.zeros((RAY_BLOCKS, TILE), jnp.float32)
    total, unused = lax.scan(step, start, (tiles, voxel_index, ray_index))
    return total


def backproject(values, tiles, voxel_index, ray_index):
    def step(total, item):
        block, vox_rows, ray_rows = item
        part = jnp.einsum("tab,ta->tb", block, jnp.take(values, ray_rows, axis=0), precision=lax.Precision.HIGHEST)
        return total + jax.ops.segment_sum(part, vox_rows, num_segments=VOXEL_TILES), None

    start = jnp.zeros((VOXEL_TILES, TILE), jnp.float32)
    total, unused = lax.scan(step, start, (tiles, voxel_index, ray_index))
    return total


def reference(tile_values, tile_vox, tile_slot, slot_block, ray_data):
    tiles = tile_values.reshape(RANKS, TILES_DEV, TILE, TILE)
    voxel_index, ray_index = tile_maps(tile_vox, tile_slot, slot_block)
    solution = jnp.zeros((VOXEL_TILES, TILE), jnp.float32)
    ray_residual = ray_data
    normal_residual = backproject(ray_residual, tiles, voxel_index, ray_index)
    norm_now = jnp.sum(normal_residual * normal_residual)
    direction = normal_residual
    for count in range(ITERS):
        image = project(direction, tiles, voxel_index, ray_index)
        step_size = norm_now / jnp.sum(image * image)
        solution = solution + step_size * direction
        ray_residual = ray_residual - step_size * image
        normal_residual = backproject(ray_residual, tiles, voxel_index, ray_index)
        if count + 1 < ITERS:
            norm_next = jnp.sum(normal_residual * normal_residual)
            direction = normal_residual + (norm_next / norm_now) * direction
            norm_now = norm_next
    return solution, ray_residual, normal_residual
```

```python
import jax
import jax.numpy as jnp
from jax import lax
from jax.experimental import pallas as pl
from jax.experimental.pallas import tpu as pltpu
from jax.sharding import PartitionSpec as P

TILE = 128
VT_DEV = 256
CAP = 4
N_VOX = 32
N_ROW = 8
PAD = 8
HEAD = CAP
EXCH = TILE + 8

F32 = jnp.float32
BF16 = jnp.bfloat16


def iota(shape, dim):
    return lax.broadcasted_iota(jnp.int32, shape, dim)


def select_rows(choice, values, transposed=False):
    high = values.astype(BF16)
    rest = values - high.astype(F32)
    middle = rest.astype(BF16)
    low = (rest - middle.astype(F32)).astype(BF16)
    total = None
    for term in (low, middle, high):
        if transposed:
            part = lax.dot_general(term, choice, (((1,), (0,)), ((), ())), preferred_element_type=F32)
        else:
            part = lax.dot_general(choice, term, (((1,), (0,)), ((), ())), preferred_element_type=F32)
        total = part if total is None else total + part
    return total


def back_tiles(tiles_ref, weight_ref):
    def step(index, total):
        for inner in range(8):
            ray = index * 8 + inner
            total = total + tiles_ref[ray] * weight_ref[pl.ds(ray, 1), :]
        return total

    return lax.fori_loop(0, TILE // 8, step, jnp.zeros((TILE, TILE), F32))


def write_exchange(exchange_ref, partial, tile_vox_row, scalar):
    rows = jnp.transpose(partial)
    sub, lane = iota((8, TILE), 0), iota((8, TILE), 1)
    tail = jnp.where(sub == 0, jnp.broadcast_to(tile_vox_row.astype(F32), (8, TILE)), 0.0)
    tail = tail + jnp.where((sub == 1) & (lane == 0), scalar, 0.0)
    for target in range(N_ROW):
        exchange_ref[target, 0:TILE, :] = rows
        exchange_ref[target, TILE:EXCH, :] = tail


def back_first_kernel(dense_ref, whole_ref, tiles_ref, tile_vox_ref, exchange_ref, picked_ref, weight_ref):
    for tile in range(TILE):
        picked_ref[tile : tile + 1, :] = whole_ref[pl.ds(dense_ref[tile], 1), :]
    weight_ref[...] = jnp.transpose(picked_ref[...])
    partial = back_tiles(tiles_ref, weight_ref)
    write_exchange(exchange_ref, partial, tile_vox_ref[...], 0.0)


def back_kernel(received_ref, tiles_ref, slot_ref, tile_vox_ref, exchange_ref, weight_ref):
    received = received_ref[...]
    rows = N_VOX * PAD
    sub, lane = iota((rows, TILE), 0), iota((rows, TILE), 1)
    choice = jnp.where(sub == slot_ref[...], 1.0, 0.0).astype(BF16)
    weight_ref[...] = select_rows(choice, jnp.transpose(received), transposed=True)
    square = jnp.sum(jnp.where((sub % PAD == HEAD) & (lane == 0), received, 0.0))
    partial = back_tiles(tiles_ref, weight_ref)
    write_exchange(exchange_ref, partial, tile_vox_ref[...], square)


def gather_field(received_ref):
    field = jnp.zeros((VT_DEV, TILE), F32)
    scalar = 0.0
    sub, lane = iota((8, TILE), 0), iota((8, TILE), 1)
    for source in range(N_ROW):
        where = received_ref[source, TILE : TILE + 1, :].astype(jnp.int32)
        choice = jnp.where(iota((VT_DEV, TILE), 0) == where, 1.0, 0.0).astype(BF16)
        field = field + select_rows(choice, received_ref[source, 0:TILE, :])
        tail = received_ref[source, TILE:EXCH, :]
        scalar = scalar + jnp.sum(jnp.where((sub == 1) & (lane == 0), tail, 0.0))
    return field, scalar


def forward_tiles(field, tiles_ref, slot_ref, tile_vox_ref, extra_ref, payload_ref, sums_ref):
    choice = jnp.where(iota((VT_DEV, TILE), 0) == tile_vox_ref[...], 1.0, 0.0).astype(BF16)
    values = select_rows(choice, jnp.transpose(field), transposed=True)

    def step(index, unused):
        for inner in range(8):
            ray = index * 8 + inner
            product = tiles_ref[ray] * values
            sums_ref[pl.ds(pl.multiple_of(ray * 8, 8), 8), :] = jnp.sum(product.reshape(TILE // 8, 8, TILE), axis=0)
        return unused

    lax.fori_loop(0, TILE // 8, step, 0)
    rays = sums_ref[pl.ds(0, TILE, stride=8), :]
    for inner in range(1, 8):
        rays = rays + sums_ref[pl.ds(inner, TILE, stride=8), :]
    rows = N_VOX * PAD
    sub, lane = iota((rows, TILE), 0), iota((rows, TILE), 1)
    choice = jnp.where(sub == slot_ref[...], 1.0, 0.0).astype(BF16)
    square = jnp.sum(field * field)
    head = extra_ref[...] + jnp.where((sub % PAD == HEAD) & (lane == CAP), square, 0.0)
    payload_ref[...] = select_rows(choice, jnp.transpose(rays)) + head


def forward_first_kernel(received_ref, tiles_ref, slot_ref, tile_vox_ref, extra_ref, payload_ref, normal_ref, sums_ref):
    field, unused = gather_field(received_ref)
    normal_ref[...] = field
    forward_tiles(field, tiles_ref, slot_ref, tile_vox_ref, extra_ref, payload_ref, sums_ref)


def forward_kernel(
    received_ref, tiles_ref, slot_ref, tile_vox_ref, extra_ref, normal0_ref, gamma_ref,
    payload_ref, normal_ref, step_ref, sums_ref,
):
    field, square = gather_field(received_ref)
    step_size = gamma_ref[...] / square
    normal = normal0_ref[...] - step_size[0:1, :] * field
    normal_ref[...] = normal
    step_ref[...] = step_size
    forward_tiles(normal, tiles_ref, slot_ref, tile_vox_ref, extra_ref, payload_ref, sums_ref)


def owner_parts(received_ref):
    received = received_ref[...]
    rows = N_VOX * PAD
    blocks = received.reshape(N_VOX, PAD, TILE)
    head = jnp.broadcast_to(blocks[:, HEAD : HEAD + 1, :], (N_VOX, PAD, TILE)).reshape(rows, TILE)
    sub, lane = iota((rows, TILE), 0), iota((rows, TILE), 1)
    place = sub % PAD
    column = jnp.sum(jnp.where((lane == place) & (place < CAP), head, 0.0), axis=1, keepdims=True)
    hit = (column.astype(jnp.int32) == lane) & (place < CAP)
    choice = jnp.where(hit, 1.0, 0.0)
    total = select_rows(jnp.transpose(choice).astype(BF16), received)
    gamma = jnp.sum(jnp.where((place == HEAD) & (lane == CAP), received, 0.0))
    return choice.astype(BF16), total, gamma


def write_owner(choice, image, owned, payload_ref):
    rows = N_VOX * PAD
    sub, lane = iota((rows, TILE), 0), iota((rows, TILE), 1)
    own_rows = iota((TILE, TILE), 0) < owned
    square = jnp.sum(jnp.where(own_rows, image * image, 0.0))
    head = jnp.where((sub % PAD == HEAD) & (lane == 0), square, 0.0)
    payload_ref[...] = select_rows(choice, image) + head


def owner_first_kernel(received_ref, payload_ref, image_ref, gamma_ref):
    choice, image, gamma = owner_parts(received_ref)
    owned = image_ref.shape[0]
    image_ref[...] = image[0:owned, :]
    gamma_ref[...] = jnp.full((8, TILE), gamma, F32)
    write_owner(choice, image, owned, payload_ref)


def owner_kernel(received_ref, image0_ref, gamma0_ref, payload_ref, image_ref, gamma_ref):
    choice, image, gamma = owner_parts(received_ref)
    owned = image_ref.shape[0]
    now = jnp.full((8, TILE), gamma, F32)
    ratio = now / gamma0_ref[...]
    gamma_ref[...] = now
    lower = image[0:owned, :] + ratio[0:1, :] * image0_ref[...]
    image_ref[...] = lower
    image = jnp.concatenate([lower, jnp.zeros((TILE - owned, TILE), F32)], axis=0)
    write_owner(choice, image, owned, payload_ref)


def last_kernel(
    received_ref, normal0_ref, normal1_ref, gamma0_ref, gamma1_ref, step0_ref, image0_ref, image1_ref, ray_ref,
    solution_ref, residual_ref, normal_ref,
):
    field, square = gather_field(received_ref)
    ratio = (gamma1_ref[...] / gamma0_ref[...])[0:1, :]
    step0 = step0_ref[0:1, :]
    step1 = (gamma1_ref[...] / square)[0:1, :]
    normal0, normal1 = normal0_ref[...], normal1_ref[...]
    direction = normal1 + ratio * normal0
    solution_ref[...] = step0 * normal0 + step1 * direction
    normal_ref[...] = normal1 - step1 * field
    residual_ref[...] = ray_ref[...] - step0 * image0_ref[...] - step1 * image1_ref[...]


def call(kernel, outs, scratch, args, smem=0):
    spec = pl.BlockSpec(memory_space=pltpu.VMEM)
    specs = [pl.BlockSpec(memory_space=pltpu.SMEM)] * smem + [spec] * (len(args) - smem)
    return pl.pallas_call(
        kernel,
        out_shape=[jax.ShapeDtypeStruct(shape, F32) for shape in outs],
        in_specs=specs,
        out_specs=[spec] * len(outs),
        scratch_shapes=[pltpu.VMEM(shape, F32) for shape in scratch],
        compiler_params=pltpu.CompilerParams(vmem_limit_bytes=24 * 1024 * 1024),
    )(*args)


def local(tile_values, tile_vox, tile_slot, slot_block, ray_data):
    owned = ray_data.shape[0]
    send_map = slot_block[0]
    dense_index = tile_slot // CAP * owned + jnp.take(send_map, tile_slot, axis=0)
    slot_row = (tile_slot // CAP * PAD + tile_slot % CAP).reshape(1, TILE)
    vox_row = tile_vox.reshape(1, TILE)
    extra = jnp.pad(
        send_map.astype(F32).reshape(N_VOX, 1, CAP), ((0, 0), (HEAD, PAD - HEAD - 1), (0, TILE - CAP))
    ).reshape(N_VOX * PAD, TILE)

    block = (TILE, TILE)
    sent = (N_VOX * PAD, TILE)
    field = (VT_DEV, TILE)
    scalar = (8, TILE)
    exchange = (N_ROW, EXCH, TILE)
    rays = (owned, TILE)

    def over_vox(array):
        return lax.all_to_all(array, "vox", 0, 0, tiled=True)

    def over_row(array):
        return lax.all_to_all(array, "row", 0, 0, tiled=True)

    copies = jnp.broadcast_to(ray_data[None], (N_VOX, owned, TILE)).reshape(N_VOX * owned, TILE)
    whole = over_vox(copies)
    tiles = jnp.transpose(tile_values, (1, 2, 0))

    (parts,) = call(back_first_kernel, [exchange], [block, block], (dense_index, whole, tiles, vox_row), smem=1)
    parts = over_row(parts)
    payload, normal0 = call(
        forward_first_kernel, [sent, field], [(TILE * 8, TILE)], (parts, tiles, slot_row, vox_row, extra)
    )
    payload, image0, gamma0 = call(owner_first_kernel, [sent, rays, scalar], [], (over_vox(payload),))
    (parts,) = call(back_kernel, [exchange], [block], (over_vox(payload), tiles, slot_row, vox_row))
    parts = over_row(parts)
    payload, normal1, step0 = call(
        forward_kernel,
        [sent, field, scalar],
        [(TILE * 8, TILE)],
        (parts, tiles, slot_row, vox_row, extra, normal0, gamma0),
    )
    payload, image1, gamma1 = call(owner_kernel, [sent, rays, scalar], [], (over_vox(payload), image0, gamma0))
    (parts,) = call(back_kernel, [exchange], [block], (over_vox(payload), tiles, slot_row, vox_row))
    parts = over_row(parts)
    return tuple(
        call(
            last_kernel,
            [field, rays, field],
            [],
            (parts, normal0, normal1, gamma0, gamma1, step0, image0, image1, ray_data),
        )
    )


def solution(mesh):
    return jax.shard_map(
        local,
        mesh=mesh,
        in_specs=(
            P(("vox", "row"), None, None),
            P(("vox", "row")),
            P(("vox", "row")),
            P(("vox", "row"), None),
            P(("vox", "row"), None),
        ),
        out_specs=(P("vox", None), P(("vox", "row"), None), P("vox", None)),
        check_vma=False,
    )
```

```python
import functools

import jax
import jax.numpy as jnp
from jax import lax
from jax.experimental import pallas as pl
from jax.experimental.pallas import tpu as pltpu
from jax.sharding import PartitionSpec as P

TILE = 128
VT_DEV = 256
CAP = 4
N_VOX = 32
N_ROW = 8
CORES = 2
CHIPS = N_VOX // CORES
CHUNKS = 8
PAD = 8
MAP = CAP
NORM = CAP + 1
SENT = N_VOX * PAD
PART = TILE + 8
SUM = VT_DEV + 8

F32 = jnp.float32
BF16 = jnp.bfloat16


def iota(shape, dim):
    return lax.broadcasted_iota(jnp.int32, shape, dim)


def select_rows(choice, values):
    high = values.astype(BF16)
    rest = values - high.astype(F32)
    middle = rest.astype(BF16)
    low = (rest - middle.astype(F32)).astype(BF16)
    total = jnp.dot(choice, low, preferred_element_type=F32)
    total = total + jnp.dot(choice, middle, preferred_element_type=F32)
    return total + jnp.dot(choice, high, preferred_element_type=F32)


def select_columns(values, choice):
    high = values.astype(BF16)
    rest = values - high.astype(F32)
    middle = rest.astype(BF16)
    low = (rest - middle.astype(F32)).astype(BF16)
    total = jnp.dot(low, choice, preferred_element_type=F32)
    total = total + jnp.dot(middle, choice, preferred_element_type=F32)
    return total + jnp.dot(high, choice, preferred_element_type=F32)


def one_hot(rows, index):
    return jnp.where(iota((rows, TILE), 0) == index, 1.0, 0.0).astype(BF16)


def copies_kernel(ray_hbm, copies_ref, ray_ref, sem):
    move = pltpu.make_async_copy(ray_hbm, ray_ref, sem)
    move.start()
    move.wait()
    owned = ray_ref.shape[0]
    rays = ray_ref[...]
    for chip in range(CHIPS):
        copies_ref[chip * owned : (chip + 1) * owned, :] = rays


def index_kernel(slot_ref, map_ref, row_ref, extra_ref, index_ref, *, owned):
    slot = slot_ref[...]
    target, place = lax.shift_right_logical(slot, 2), slot & (CAP - 1)
    row_ref[...] = target * PAD + place
    sub, lane = iota((TILE, TILE), 0), iota((TILE, TILE), 1)
    column = jnp.transpose(jnp.broadcast_to(map_ref[...].astype(F32), (TILE, TILE)))
    block = jnp.sum(jnp.where(sub == slot, column, 0.0), axis=0, keepdims=True).astype(jnp.int32)
    mine = lax.axis_index("vox") & (CORES - 1)
    other = (target & (CORES - 1)) ^ mine
    index_ref[...] = (other * CHIPS + lax.shift_right_logical(target, 1)) * owned + block
    values = jnp.where((sub & (CAP - 1)) == lane, column, 0.0).astype(BF16)
    sub, lane = iota((SENT, TILE), 0), iota((SENT, TILE), 1)
    hit = ((sub & (PAD - 1)) == MAP) & (lax.shift_right_logical(lane, 2) == lax.shift_right_logical(sub, 3))
    choice = jnp.where(hit, 1.0, 0.0).astype(BF16)
    extra_ref[...] = jnp.dot(choice, values, preferred_element_type=F32)


def relay_kernel(natural_ref, tiles_ref):
    def step(index, unused):
        block = natural_ref[:, pl.ds(pl.multiple_of(index * 8, 8), 8), :]
        block = jnp.swapaxes(block, 0, 1)
        for inner in range(8):
            tiles_ref[index * 8 + inner] = jnp.transpose(block[inner])
        return unused

    lax.fori_loop(0, TILE // 8, step, 0)


def back_tiles(tiles_ref, weight_ref):
    def step(index, total):
        for inner in range(8):
            ray = index * 8 + inner
            total = total + tiles_ref[ray] * weight_ref[pl.ds(ray, 1), :]
        return total

    return lax.fori_loop(0, TILE // 8, step, jnp.zeros((TILE, TILE), F32))


def write_tail(part_ref, vox_row, square):
    sub = iota((8, TILE), 0)
    tail = jnp.where(sub == 0, jnp.broadcast_to(vox_row.astype(F32), (8, TILE)), 0.0)
    part_ref[TILE:PART, :] = tail + jnp.where(sub == 1, jnp.broadcast_to(square, (8, TILE)), 0.0)


def back_first_kernel(index_ref, tiles_hbm, same_ref, other_ref, vox_ref, part_ref, natural_ref, picked_ref, sems):
    size = TILE // CHUNKS
    moves = []
    for chunk in range(CHUNKS):
        where = pl.ds(chunk * size, size)
        moves.append(pltpu.make_async_copy(tiles_hbm.at[where], natural_ref.at[where], sems.at[chunk]))
    for move in moves:
        move.start()
    half = same_ref.shape[0]
    for tile in range(TILE):
        index = index_ref[0, tile]
        here = index < half
        row = jnp.where(here, index, index - half)
        picked_ref[tile : tile + 1, :] = jnp.where(here, same_ref[pl.ds(row, 1), :], other_ref[pl.ds(row, 1), :])
    weight = jnp.transpose(picked_ref[...])
    write_tail(part_ref, vox_ref[...], jnp.zeros((1, TILE), F32))
    for group in range(TILE // 8):
        if group * 8 % size == 0:
            moves[group * 8 // size].wait()
        rows = []
        for tile in range(group * 8, group * 8 + 8):
            rows.append(jnp.sum(natural_ref[tile] * weight[:, tile : tile + 1], axis=0, keepdims=True))
        part_ref[group * 8 : group * 8 + 8, :] = jnp.concatenate(rows, axis=0)


def back_kernel(received_ref, tiles_ref, row_ref, vox_ref, part_ref, weight_ref):
    received = received_ref[...]
    weight_ref[...] = select_columns(jnp.transpose(received), one_hot(SENT, row_ref[...]))
    square = jnp.sum(received.reshape(N_VOX, PAD, TILE), axis=0)[NORM : NORM + 1, :]
    part_ref[0:TILE, :] = jnp.transpose(back_tiles(tiles_ref, weight_ref))
    write_tail(part_ref, vox_ref[...], square)


def quad_kernel(own_ref, one_ref, two_ref, three_ref, sum_ref):
    def spread(ref):
        where = ref[TILE : TILE + 1, :].astype(jnp.int32)
        return select_rows(one_hot(VT_DEV, where), ref[0:TILE, :])

    sum_ref[0:VT_DEV, :] = (spread(own_ref) + spread(one_ref)) + (spread(two_ref) + spread(three_ref))
    tail = slice(TILE, PART)
    sum_ref[VT_DEV:SUM, :] = (own_ref[tail, :] + one_ref[tail, :]) + (two_ref[tail, :] + three_ref[tail, :])


def whole_sum(near_ref, far_ref):
    field = near_ref[0:VT_DEV, :] + far_ref[0:VT_DEV, :]
    tail = near_ref[VT_DEV:SUM, :] + far_ref[VT_DEV:SUM, :]
    return field, jnp.sum(tail[1:2, :], axis=1, keepdims=True)


def forward_tiles(field, tiles_ref, row_ref, vox_ref, extra_ref, payload_ref, sums_ref):
    values = select_columns(jnp.transpose(field), one_hot(VT_DEV, vox_ref[...]))

    def step(index, unused):
        for inner in range(8):
            ray = index * 8 + inner
            product = tiles_ref[ray] * values
            sums_ref[pl.ds(pl.multiple_of(ray * 8, 8), 8), :] = jnp.sum(product.reshape(TILE // 8, 8, TILE), axis=0)
        return unused

    lax.fori_loop(0, TILE // 8, step, 0)
    rays = sums_ref[pl.ds(0, TILE, stride=8), :]
    for inner in range(1, 8):
        rays = rays + sums_ref[pl.ds(inner, TILE, stride=8), :]
    square = jnp.sum(field * field, axis=0, keepdims=True)
    head = jnp.where((iota((SENT, TILE), 0) & (PAD - 1)) == NORM, square, extra_ref[...])
    payload_ref[...] = select_rows(one_hot(SENT, row_ref[...]), jnp.transpose(rays)) + head


def forward_first_kernel(near_ref, far_ref, tiles_ref, row_ref, vox_ref, extra_ref, payload_ref, normal_ref, sums_ref):
    field, unused = whole_sum(near_ref, far_ref)
    normal_ref[...] = field
    forward_tiles(field, tiles_ref, row_ref, vox_ref, extra_ref, payload_ref, sums_ref)


def forward_kernel(
    near_ref, far_ref, tiles_ref, row_ref, vox_ref, extra_ref, normal0_ref, gamma_ref,
    payload_ref, normal_ref, step_ref, sums_ref,
):
    field, square = whole_sum(near_ref, far_ref)
    step_size = gamma_ref[...] / square
    normal = normal0_ref[...] - step_size[0:1, :] * field
    normal_ref[...] = normal
    step_ref[...] = step_size
    forward_tiles(normal, tiles_ref, row_ref, vox_ref, extra_ref, payload_ref, sums_ref)


def owner_parts(received_ref):
    received = received_ref[...]
    blocks = received.reshape(N_VOX, PAD, TILE)
    head = jnp.broadcast_to(blocks[:, MAP : MAP + 1, :], (N_VOX, PAD, TILE)).reshape(SENT, TILE)
    place, lane = iota((SENT, TILE), 0) & (PAD - 1), iota((SENT, TILE), 1)
    column = jnp.sum(jnp.where((lane == place) & (place < CAP), head, 0.0), axis=1, keepdims=True)
    hit = (column.astype(jnp.int32) == lane) & (place < CAP)
    choice = jnp.where(hit, 1.0, 0.0)
    image = select_rows(jnp.transpose(choice).astype(BF16), received)
    gamma = jnp.sum(jnp.sum(blocks, axis=0)[NORM : NORM + 1, :], axis=1, keepdims=True)
    return choice.astype(BF16), image, jnp.broadcast_to(gamma, (8, TILE))


def write_owner(choice, image, owned, payload_ref):
    square = jnp.where(iota((TILE, TILE), 0) < owned, image * image, 0.0)
    square = jnp.sum(square, axis=0, keepdims=True)
    head = jnp.where((iota((SENT, TILE), 0) & (PAD - 1)) == NORM, square, 0.0)
    payload_ref[...] = select_rows(choice, image) + head


def owner_first_kernel(received_ref, payload_ref, image_ref, gamma_ref):
    choice, image, gamma = owner_parts(received_ref)
    owned = image_ref.shape[0]
    image_ref[...] = image[0:owned, :]
    gamma_ref[...] = gamma
    write_owner(choice, image, owned, payload_ref)


def owner_kernel(received_ref, image0_ref, gamma0_ref, payload_ref, image_ref, gamma_ref):
    choice, image, gamma = owner_parts(received_ref)
    owned = image_ref.shape[0]
    ratio = gamma / gamma0_ref[...]
    gamma_ref[...] = gamma
    lower = image[0:owned, :] + ratio[0:1, :] * image0_ref[...]
    image_ref[...] = lower
    image = jnp.concatenate([lower, jnp.zeros((TILE - owned, TILE), F32)], axis=0)
    write_owner(choice, image, owned, payload_ref)


def last_kernel(
    near_ref, far_ref, normal0_ref, normal1_ref, gamma0_ref, gamma1_ref, step0_ref, image0_ref, image1_ref, ray_ref,
    solution_ref, residual_ref, normal_ref,
):
    field, square = whole_sum(near_ref, far_ref)
    ratio = (gamma1_ref[...] / gamma0_ref[...])[0:1, :]
    step0 = step0_ref[0:1, :]
    step1 = (gamma1_ref[...] / square)[0:1, :]
    normal0, normal1 = normal0_ref[...], normal1_ref[...]
    direction = normal1 + ratio * normal0
    solution_ref[...] = step0 * normal0 + step1 * direction
    normal_ref[...] = normal1 - step1 * field
    residual_ref[...] = ray_ref[...] - step0 * image0_ref[...] - step1 * image1_ref[...]


def call(kernel, outs, scratch, args, smem=0, hbm=0, cost=None, limit=24):
    vmem = pl.BlockSpec(memory_space=pltpu.VMEM)
    specs = [pl.BlockSpec(memory_space=pltpu.SMEM)] * smem + [pl.BlockSpec(memory_space=pl.ANY)] * hbm
    outs = [out if isinstance(out, jax.ShapeDtypeStruct) else jax.ShapeDtypeStruct(out, F32) for out in outs]
    return pl.pallas_call(
        kernel,
        out_shape=outs,
        in_specs=specs + [vmem] * (len(args) - smem - hbm),
        out_specs=[vmem] * len(outs),
        scratch_shapes=[pltpu.VMEM(shape, F32) if isinstance(shape, tuple) else shape for shape in scratch],
        cost_estimate=cost,
        compiler_params=pltpu.CompilerParams(vmem_limit_bytes=limit * 1024 * 1024),
    )(*args)


def local(tile_values, tile_vox, tile_slot, slot_block, ray_data):
    owned = ray_data.shape[0]
    block = (TILE, TILE)
    sent = (SENT, TILE)
    field = (VT_DEV, TILE)
    scalar = (8, TILE)
    part = (PART, TILE)
    sums = (TILE * 8, TILE)
    rays = (owned, TILE)
    indices = jax.ShapeDtypeStruct((1, TILE), jnp.int32)

    def over_vox(array):
        return lax.all_to_all(array, "vox", 0, 0, tiled=True)

    def across(array, distance):
        return lax.ppermute(array, "row", [(index, index ^ distance) for index in range(N_ROW)])

    def quad(own):
        others = [across(own, distance) for distance in (1, 2, 3)]
        return call(quad_kernel, [(SUM, TILE)], [], (own, *others))[0]

    def over_row(own):
        near = quad(own)
        return near, across(near, 6)

    (copies,) = call(
        copies_kernel,
        [(CHIPS * owned, TILE)],
        [rays, pltpu.SemaphoreType.DMA],
        (ray_data,),
        hbm=1,
        limit=60,
    )
    chips = [[chip * CORES + core for chip in range(CHIPS)] for core in range(CORES)]
    same = lax.all_to_all(copies, "vox", 0, 0, tiled=True, axis_index_groups=chips)
    same, tile_vox, tile_slot, slot_block = lax.optimization_barrier((same, tile_vox, tile_slot, slot_block))
    other = lax.ppermute(same, "vox", [(device, device ^ 1) for device in range(N_VOX)])
    vox_row = tile_vox.reshape(1, TILE)
    slot_row, extra, index = call(
        functools.partial(index_kernel, owned=owned),
        [indices, sent, indices],
        [],
        (tile_slot.reshape(1, TILE), slot_block),
    )
    parts, natural = call(
        back_first_kernel,
        [part, (TILE, TILE, TILE)],
        [block, pltpu.SemaphoreType.DMA((CHUNKS,))],
        (index, tile_values, same, other, vox_row),
        smem=1,
        hbm=1,
        limit=42,
    )
    near = quad(parts)
    near, natural = lax.optimization_barrier((near, natural))
    far = across(near, 6)
    (tiles,) = call(
        relay_kernel,
        [(TILE, TILE, TILE)],
        [],
        (natural,),
        cost=pl.CostEstimate(flops=0, bytes_accessed=2**24, transcendentals=0),
    )
    payload, normal0 = call(
        forward_first_kernel, [sent, field], [sums], (near, far, tiles, slot_row, vox_row, extra)
    )
    payload, image0, gamma0 = call(owner_first_kernel, [sent, rays, scalar], [], (over_vox(payload),))
    (parts,) = call(back_kernel, [part], [block], (over_vox(payload), tiles, slot_row, vox_row))
    near, far = over_row(parts)
    payload, normal1, step0 = call(
        forward_kernel,
        [sent, field, scalar],
        [sums],
        (near, far, tiles, slot_row, vox_row, extra, normal0, gamma0),
    )
    payload, image1, gamma1 = call(owner_kernel, [sent, rays, scalar], [], (over_vox(payload), image0, gamma0))
    (parts,) = call(back_kernel, [part], [block], (over_vox(payload), tiles, slot_row, vox_row))
    near, far = over_row(parts)
    return tuple(
        call(
            last_kernel,
            [field, rays, field],
            [],
            (near, far, normal0, normal1, gamma0, gamma1, step0, image0, image1, ray_data),
        )
    )


def solution(mesh):
    return jax.shard_map(
        local,
        mesh=mesh,
        in_specs=(
            P(("vox", "row"), None, None),
            P(("vox", "row")),
            P(("vox", "row")),
            P(("vox", "row"), None),
            P(("vox", "row"), None),
        ),
        out_specs=(P("vox", None), P(("vox", "row"), None), P("vox", None)),
        check_vma=False,
    )
```

```python
import jax
import jax.numpy as jnp
from jax import lax
from jax.experimental import pallas as pl
from jax.experimental.pallas import tpu as pltpu
from jax.sharding import PartitionSpec as P

TILE = 128
VT_DEV = 256
CAP = 4
N_VOX = 32
N_ROW = 8
CORES = 2
CHIPS = N_VOX // CORES
CHUNKS = 8
PAD = 8
MAP = CAP
NORM = CAP + 1
NORM2 = CAP + 2
SENT = N_VOX * PAD
PART = TILE + 8
SUM = VT_DEV + 8
IDS, IMAGE, GAMMA, CROSS = 0, 1, 2, 3

F32 = jnp.float32
BF16 = jnp.bfloat16


def iota(shape, dim):
    return lax.broadcasted_iota(jnp.int32, shape, dim)


def select_rows(choice, values):
    high = values.astype(BF16)
    rest = values - high.astype(F32)
    middle = rest.astype(BF16)
    low = (rest - middle.astype(F32)).astype(BF16)
    total = jnp.dot(choice, low, preferred_element_type=F32)
    total = total + jnp.dot(choice, middle, preferred_element_type=F32)
    return total + jnp.dot(choice, high, preferred_element_type=F32)


def select_columns(values, choice):
    high = values.astype(BF16)
    rest = values - high.astype(F32)
    middle = rest.astype(BF16)
    low = (rest - middle.astype(F32)).astype(BF16)
    total = jnp.dot(low, choice, preferred_element_type=F32)
    total = total + jnp.dot(middle, choice, preferred_element_type=F32)
    return total + jnp.dot(high, choice, preferred_element_type=F32)


def one_hot(rows, index):
    return jnp.where(iota((rows, TILE), 0) == index, 1.0, 0.0).astype(BF16)


def copies_kernel(ray_ref, copies_ref):
    owned = ray_ref.shape[0]
    rays = ray_ref[...]
    for chip in range(CHIPS):
        copies_ref[chip * owned : (chip + 1) * owned, :] = rays


def pack_kernel(slot_ref, map_ref, vox_ref, pack_ref):
    pack_ref[...] = jnp.zeros_like(pack_ref)
    pack_ref[0:1, :] = slot_ref[...]
    pack_ref[1:2, :] = map_ref[...]
    pack_ref[2:3, :] = vox_ref[...]


def relay_kernel(natural_ref, tiles_ref):
    def step(index, unused):
        block = natural_ref[:, pl.ds(pl.multiple_of(index * 8, 8), 8), :]
        block = jnp.swapaxes(block, 0, 1)
        for inner in range(8):
            tiles_ref[index * 8 + inner] = jnp.transpose(block[inner])
        return unused

    lax.fori_loop(0, TILE // 8, step, 0)


def back_tiles(tiles_ref, weight_ref):
    def step(index, total):
        for inner in range(8):
            ray = index * 8 + inner
            total = total + tiles_ref[ray] * weight_ref[pl.ds(ray, 1), :]
        return total

    return lax.fori_loop(0, TILE // 8, step, jnp.zeros((TILE, TILE), F32))


def write_tail(part_ref, vox_row, image, gamma, cross):
    sub = iota((8, TILE), 0)
    tail = jnp.where(sub == IDS, jnp.broadcast_to(vox_row.astype(F32), (8, TILE)), 0.0)
    for place, row in ((IMAGE, image), (GAMMA, gamma), (CROSS, cross)):
        if row is not None:
            tail = tail + jnp.where(sub == place, jnp.broadcast_to(row, (8, TILE)), 0.0)
    part_ref[TILE:PART, :] = tail


def back_first_kernel(
    tiles_hbm, same_ref, other_ref, pack_ref,
    part_ref, share_ref, natural_ref, row_ref, vox_ref, extra_ref, ids_ref,
    picked_ref, index_ref, place_ref, sems,
):
    size = TILE // CHUNKS
    moves = []
    for chunk in range(CHUNKS):
        where = pl.ds(chunk * size, size)
        moves.append(pltpu.make_async_copy(tiles_hbm.at[where], natural_ref.at[where], sems.at[chunk]))
    for move in moves:
        move.start()

    owned = same_ref.shape[0] // CHIPS
    slot, vox = pack_ref[0:1, :], pack_ref[2:3, :]
    target, place = lax.shift_right_logical(slot, 2), slot & (CAP - 1)
    sub, lane = iota((TILE, TILE), 0), iota((TILE, TILE), 1)
    column = jnp.transpose(jnp.broadcast_to(pack_ref[1:2, :].astype(F32), (TILE, TILE)))
    block = jnp.sum(jnp.where(sub == slot, column, 0.0), axis=0, keepdims=True).astype(jnp.int32)
    mine = lax.axis_index("vox") & (CORES - 1)
    other = (target & (CORES - 1)) ^ mine
    index_ref[...] = (other * CHIPS + lax.shift_right_logical(target, 1)) * owned + block
    move = pltpu.make_async_copy(index_ref, place_ref, sems.at[CHUNKS])
    move.start()

    row_ref[...] = target * PAD + place
    vox_ref[...] = vox
    ids_ref[...] = jnp.broadcast_to(vox.astype(F32), (8, TILE))
    write_tail(part_ref, vox, None, None, None)
    values = jnp.where((sub & (CAP - 1)) == lane, column, 0.0).astype(BF16)
    sub, lane = iota((SENT, TILE), 0), iota((SENT, TILE), 1)
    hit = ((sub & (PAD - 1)) == MAP) & (lax.shift_right_logical(lane, 2) == lax.shift_right_logical(sub, 3))
    choice = jnp.where(hit, 1.0, 0.0).astype(BF16)
    extra_ref[...] = jnp.dot(choice, values, preferred_element_type=F32)

    move.wait()
    half = same_ref.shape[0]
    for tile in range(TILE):
        index = place_ref[0, tile]
        here = index < half
        row = jnp.where(here, index, index - half)
        picked_ref[tile : tile + 1, :] = jnp.where(here, same_ref[pl.ds(row, 1), :], other_ref[pl.ds(row, 1), :])
    weight = jnp.transpose(picked_ref[...])
    for group in range(TILE // 8):
        if group * 8 % size == 0:
            moves[group * 8 // size].wait()
        rows = []
        for tile in range(group * 8, group * 8 + 8):
            rows.append(jnp.sum(natural_ref[tile] * weight[:, tile : tile + 1], axis=0, keepdims=True))
        part_ref[group * 8 : group * 8 + 8, :] = jnp.concatenate(rows, axis=0)
    share_ref[...] = jnp.transpose(part_ref[0:TILE, :])


def back_share(received_ref, tiles_ref, row_ref, vox_ref, gamma_ref, part_ref, weight_ref):
    received = received_ref[...]
    weight_ref[...] = select_columns(jnp.transpose(received), one_hot(SENT, row_ref[...]))
    heads = jnp.sum(received.reshape(N_VOX, PAD, TILE), axis=0)
    share = back_tiles(tiles_ref, weight_ref)
    part_ref[0:TILE, :] = jnp.transpose(share)
    write_tail(part_ref, vox_ref[...], heads[NORM : NORM + 1, :], gamma_ref[0:1, :], heads[NORM2 : NORM2 + 1, :])
    return share


def back_kernel(received_ref, tiles_ref, row_ref, vox_ref, gamma_ref, part_ref, share_ref, weight_ref):
    share_ref[...] = back_share(received_ref, tiles_ref, row_ref, vox_ref, gamma_ref, part_ref, weight_ref)


def back_last_kernel(received_ref, tiles_ref, row_ref, vox_ref, gamma_ref, part_ref, weight_ref):
    back_share(received_ref, tiles_ref, row_ref, vox_ref, gamma_ref, part_ref, weight_ref)


def quad_sum(own_ref, one_ref, two_ref, three_ref):
    def spread(ref):
        where = ref[TILE + IDS : TILE + IDS + 1, :].astype(jnp.int32)
        return select_rows(one_hot(VT_DEV, where), ref[0:TILE, :])

    field = (spread(own_ref) + spread(one_ref)) + (spread(two_ref) + spread(three_ref))
    tail = slice(TILE, PART)
    return field, (own_ref[tail, :] + one_ref[tail, :]) + (two_ref[tail, :] + three_ref[tail, :])


def read_tiles(field, tail, own_ref, ids_ref, mine_ref, send_ref):
    here = one_hot(VT_DEV, own_ref[TILE + IDS : TILE + IDS + 1, :].astype(jnp.int32))
    there = one_hot(VT_DEV, ids_ref[0:1, :].astype(jnp.int32))
    both = select_columns(jnp.transpose(field), jnp.concatenate([here, there], axis=1))
    mine_ref[...] = both[:, 0:TILE]
    send_ref[0:TILE, :] = both[:, TILE : 2 * TILE]
    send_ref[TILE:PART, :] = tail


def quad_first_kernel(own_ref, one_ref, two_ref, three_ref, ids_ref, near_ref, mine_ref, send_ref):
    field, tail = quad_sum(own_ref, one_ref, two_ref, three_ref)
    read_tiles(field, tail, own_ref, ids_ref, mine_ref, send_ref)
    near_ref[...] = field


def quad_kernel(own_ref, one_ref, two_ref, three_ref, ids_ref, before_ref, near_ref, mine_ref, send_ref):
    field, tail = quad_sum(own_ref, one_ref, two_ref, three_ref)
    read_tiles(field, tail, own_ref, ids_ref, mine_ref, send_ref)
    near_ref[0:VT_DEV, :] = before_ref[...]
    near_ref[VT_DEV:, :] = field


def quad_last_kernel(own_ref, one_ref, two_ref, three_ref, near_ref):
    field, tail = quad_sum(own_ref, one_ref, two_ref, three_ref)
    near_ref[0:VT_DEV, :] = field
    near_ref[VT_DEV:SUM, :] = tail


def forward_tiles(values, share, tiles_ref, row_ref, extra_ref, payload_ref, sums_ref):
    def step(index, unused):
        for inner in range(8):
            ray = index * 8 + inner
            product = tiles_ref[ray] * values
            sums_ref[pl.ds(pl.multiple_of(ray * 8, 8), 8), :] = jnp.sum(product.reshape(TILE // 8, 8, TILE), axis=0)
        return unused

    lax.fori_loop(0, TILE // 8, step, 0)
    rays = sums_ref[pl.ds(0, TILE, stride=8), :]
    for inner in range(1, 8):
        rays = rays + sums_ref[pl.ds(inner, TILE, stride=8), :]
    gamma = jnp.sum(values * share, axis=0, keepdims=True)
    head = jnp.where((iota((SENT, TILE), 0) & (PAD - 1)) == NORM, gamma, extra_ref[...])
    payload_ref[...] = select_rows(one_hot(SENT, row_ref[...]), jnp.transpose(rays)) + head


def forward_first_kernel(mine_ref, far_ref, share_ref, tiles_ref, row_ref, extra_ref, payload_ref, values_ref, sums_ref):
    values = mine_ref[...] + far_ref[0:TILE, :]
    values_ref[...] = values
    forward_tiles(values, share_ref[...], tiles_ref, row_ref, extra_ref, payload_ref, sums_ref)


def lane_sum(tail, place):
    return jnp.sum(tail[place : place + 1, :], axis=1, keepdims=True)


def forward_kernel(
    mine_ref, send_ref, far_ref, share_ref, values0_ref, share0_ref, tiles_ref, row_ref, extra_ref,
    payload_ref, scalars_ref, sums_ref,
):
    tail = send_ref[TILE:PART, :] + far_ref[TILE:PART, :]
    gamma, square = lane_sum(tail, GAMMA), lane_sum(tail, IMAGE)
    step = gamma / square
    sub = iota((8, TILE), 0)
    scalars_ref[...] = jnp.where(sub == 0, gamma, jnp.where(sub == 1, square, step))
    values = values0_ref[...] - step * (mine_ref[...] + far_ref[0:TILE, :])
    share = share0_ref[...] - step * share_ref[...]
    forward_tiles(values, share, tiles_ref, row_ref, extra_ref, payload_ref, sums_ref)


def owner_parts(received_ref):
    received = received_ref[...]
    blocks = received.reshape(N_VOX, PAD, TILE)
    head = jnp.broadcast_to(blocks[:, MAP : MAP + 1, :], (N_VOX, PAD, TILE)).reshape(SENT, TILE)
    place, lane = iota((SENT, TILE), 0) & (PAD - 1), iota((SENT, TILE), 1)
    column = jnp.sum(jnp.where((lane == place) & (place < CAP), head, 0.0), axis=1, keepdims=True)
    hit = (column.astype(jnp.int32) == lane) & (place < CAP)
    choice = jnp.where(hit, 1.0, 0.0)
    image = select_rows(jnp.transpose(choice).astype(BF16), received)
    gamma = jnp.sum(blocks, axis=0)[NORM : NORM + 1, :]
    return choice.astype(BF16), image, jnp.broadcast_to(gamma, (8, TILE))


def owner_first_kernel(received_ref, payload_ref, image_ref, gamma_ref):
    choice, image, gamma_ref[...] = owner_parts(received_ref)
    owned = image_ref.shape[0]
    lower = image[0:owned, :]
    image_ref[...] = lower
    square = jnp.sum(lower * lower, axis=0, keepdims=True)
    place = iota((SENT, TILE), 0) & (PAD - 1)
    payload_ref[...] = select_rows(choice, image) + jnp.where(place == NORM, square, 0.0)


def owner_kernel(received_ref, image0_ref, payload_ref, image_ref, gamma_ref):
    choice, image, gamma_ref[...] = owner_parts(received_ref)
    owned = image_ref.shape[0]
    lower = image[0:owned, :]
    image_ref[...] = lower
    square = jnp.sum(lower * lower, axis=0, keepdims=True)
    cross = jnp.sum(lower * image0_ref[...], axis=0, keepdims=True)
    place = iota((SENT, TILE), 0) & (PAD - 1)
    head = jnp.where(place == NORM, square, jnp.where(place == NORM2, cross, 0.0))
    payload_ref[...] = select_rows(choice, image) + head


def last_kernel(
    near_ref, far_ref, inner_near_ref, inner_far_ref, scalars_ref, image0_ref, image1_ref, ray_ref,
    solution_ref, residual_ref, normal_ref,
):
    tail = near_ref[VT_DEV:SUM, :] + far_ref[VT_DEV:SUM, :]
    gamma0, square0, step0 = scalars_ref[0:1, :], scalars_ref[1:2, :], scalars_ref[2:3, :]
    gamma1 = lane_sum(tail, GAMMA)
    ratio = gamma1 / gamma0
    square1 = lane_sum(tail, IMAGE) + 2.0 * ratio * lane_sum(tail, CROSS) + ratio * ratio * square0
    step1 = gamma1 / square1
    normal0 = inner_near_ref[0:VT_DEV, :] + inner_far_ref[0:VT_DEV, :]
    change0 = inner_near_ref[VT_DEV:, :] + inner_far_ref[VT_DEV:, :]
    normal1 = normal0 - step0 * change0
    change1 = near_ref[0:VT_DEV, :] + far_ref[0:VT_DEV, :] + ratio * change0
    solution_ref[...] = step0 * normal0 + step1 * (normal1 + ratio * normal0)
    normal_ref[...] = normal1 - step1 * change1
    image0 = image0_ref[...]
    residual_ref[...] = ray_ref[...] - step0 * image0 - step1 * (image1_ref[...] + ratio * image0)


def call(kernel, outs, scratch, args, hbm=0, cost=None, limit=24):
    vmem = pl.BlockSpec(memory_space=pltpu.VMEM)
    specs = [pl.BlockSpec(memory_space=pl.ANY)] * hbm
    outs = [out if isinstance(out, jax.ShapeDtypeStruct) else jax.ShapeDtypeStruct(out, F32) for out in outs]
    return pl.pallas_call(
        kernel,
        out_shape=outs,
        in_specs=specs + [vmem] * (len(args) - hbm),
        out_specs=[vmem] * len(outs),
        scratch_shapes=[pltpu.VMEM(shape, F32) if isinstance(shape, tuple) else shape for shape in scratch],
        cost_estimate=cost,
        compiler_params=pltpu.CompilerParams(vmem_limit_bytes=limit * 1024 * 1024),
    )(*args)


def local(tile_values, tile_vox, tile_slot, slot_block, ray_data):
    owned = ray_data.shape[0]
    block = (TILE, TILE)
    sent = (SENT, TILE)
    field = (VT_DEV, TILE)
    scalar = (8, TILE)
    part = (PART, TILE)
    sums = (TILE * 8, TILE)
    rays = (owned, TILE)
    indices = jax.ShapeDtypeStruct((1, TILE), jnp.int32)

    def over_vox(array):
        return lax.all_to_all(array, "vox", 0, 0, tiled=True)

    def across(array, distance):
        return lax.ppermute(array, "row", [(index, index ^ distance) for index in range(N_ROW)])

    def quad(own):
        return (own, *(across(own, distance) for distance in (1, 2, 3)))

    (copies,) = call(copies_kernel, [(CHIPS * owned, TILE)], [], (ray_data,))
    chips = [[chip * CORES + core for chip in range(CHIPS)] for core in range(CORES)]
    same = lax.all_to_all(copies, "vox", 0, 0, tiled=True, axis_index_groups=chips)
    same, tile_vox, tile_slot, slot_block = lax.optimization_barrier((same, tile_vox, tile_slot, slot_block))
    other = lax.ppermute(same, "vox", [(device, device ^ 1) for device in range(N_VOX)])
    (pack,) = call(
        pack_kernel,
        [jax.ShapeDtypeStruct(scalar, jnp.int32)],
        [],
        (tile_slot.reshape(1, TILE), slot_block, tile_vox.reshape(1, TILE)),
    )
    own, share0, natural, slot_row, vox_row, extra, ids = call(
        back_first_kernel,
        [part, block, (TILE, TILE, TILE), indices, indices, sent, scalar],
        [
            block,
            pltpu.VMEM((1, TILE), jnp.int32),
            pltpu.SMEM((1, TILE), jnp.int32),
            pltpu.SemaphoreType.DMA((CHUNKS + 1,)),
        ],
        (tile_values, same, other, pack),
        hbm=1,
        limit=42,
    )
    ids = across(ids, 6)
    near, mine, send = call(quad_first_kernel, [field, block, part], [], (*quad(own), ids))
    send, natural = lax.optimization_barrier((send, natural))
    far = across(send, 6)
    (tiles,) = call(
        relay_kernel,
        [(TILE, TILE, TILE)],
        [],
        (natural,),
        cost=pl.CostEstimate(flops=0, bytes_accessed=2**24, transcendentals=0),
    )
    payload, values0 = call(
        forward_first_kernel, [sent, block], [sums], (mine, far, share0, tiles, slot_row, extra)
    )
    payload, image0, gamma = call(owner_first_kernel, [sent, rays, scalar], [], (over_vox(payload),))
    own, share = call(back_kernel, [part, block], [block], (over_vox(payload), tiles, slot_row, vox_row, gamma))
    near, mine, send = call(
        quad_kernel, [(2 * VT_DEV, TILE), block, part], [], (*quad(own), ids, near)
    )
    far, near = lax.optimization_barrier((across(send, 6), near))
    inner_far = across(near, 6)
    payload, scalars = call(
        forward_kernel,
        [sent, scalar],
        [sums],
        (mine, send, far, share, values0, share0, tiles, slot_row, extra),
    )
    received, inner_far = lax.optimization_barrier((over_vox(payload), inner_far))
    payload, image1, gamma = call(owner_kernel, [sent, rays, scalar], [], (received, image0))
    (own,) = call(back_last_kernel, [part], [block], (over_vox(payload), tiles, slot_row, vox_row, gamma))
    (last,) = call(quad_last_kernel, [(SUM, TILE)], [], quad(own))
    return tuple(
        call(
            last_kernel,
            [field, rays, field],
            [],
            (last, across(last, 6), near, inner_far, scalars, image0, image1, ray_data),
        )
    )


def solution(mesh):
    return jax.shard_map(
        local,
        mesh=mesh,
        in_specs=(
            P(("vox", "row"), None, None),
            P(("vox", "row")),
            P(("vox", "row")),
            P(("vox", "row"), None),
            P(("vox", "row"), None),
        ),
        out_specs=(P("vox", None), P(("vox", "row"), None), P("vox", None)),
        check_vma=False,
    )
```

```python
import jax
import jax.numpy as jnp
from jax import lax
from jax.experimental import pallas as pl
from jax.experimental.pallas import tpu as pltpu
from jax.sharding import PartitionSpec as P

TILE = 128
VT_DEV = 256
CAP = 4
N_VOX = 32
N_ROW = 8
CORES = 2
CHIPS = N_VOX // CORES
CHUNKS = 8
PAD = 8
MAP = CAP
NORM, LOCAL, OTHER = CAP, CAP + 1, CAP + 2
SENT = N_VOX * PAD
PART = TILE + 8
SUM = VT_DEV + 8
IDS, IMAGE, GAMMA, CROSS = 0, 1, 2, 3

F32 = jnp.float32
BF16 = jnp.bfloat16


def iota(shape, dim):
    return lax.broadcasted_iota(jnp.int32, shape, dim)


def select_rows(choice, values):
    high = values.astype(BF16)
    middle = (values - high.astype(F32)).astype(BF16)
    total = jnp.dot(choice, middle, preferred_element_type=F32)
    return total + jnp.dot(choice, high, preferred_element_type=F32)


def select_columns(values, choice):
    high = values.astype(BF16)
    middle = (values - high.astype(F32)).astype(BF16)
    total = jnp.dot(middle, choice, preferred_element_type=F32)
    return total + jnp.dot(high, choice, preferred_element_type=F32)


def one_hot(rows, index):
    return jnp.where(iota((rows, TILE), 0) == index, 1.0, 0.0).astype(BF16)


def copies_kernel(ray_ref, copies_ref):
    owned = ray_ref.shape[0]
    rays = ray_ref[...]
    for chip in range(CHIPS):
        copies_ref[chip * owned : (chip + 1) * owned, :] = rays


def pack_kernel(slot_ref, map_ref, vox_ref, pack_ref):
    pack_ref[...] = jnp.zeros_like(pack_ref)
    pack_ref[0:1, :] = slot_ref[...]
    pack_ref[1:2, :] = map_ref[...]
    pack_ref[2:3, :] = vox_ref[...]


def relay_kernel(natural_ref, tiles_ref):
    def step(index, unused):
        block = natural_ref[:, pl.ds(pl.multiple_of(index * 8, 8), 8), :]
        block = jnp.swapaxes(block, 0, 1)
        for inner in range(8):
            tiles_ref[index * 8 + inner] = jnp.transpose(block[inner])
        return unused

    lax.fori_loop(0, TILE // 8, step, 0)


def back_tiles(tiles_ref, weight_ref):
    def step(index, total):
        for inner in range(8):
            ray = index * 8 + inner
            total = total + tiles_ref[ray] * weight_ref[pl.ds(ray, 1), :]
        return total

    return lax.fori_loop(0, TILE // 8, step, jnp.zeros((TILE, TILE), F32))


def write_tail(part_ref, vox_row, image, gamma, cross):
    sub = iota((8, TILE), 0)
    tail = jnp.where(sub == IDS, jnp.broadcast_to(vox_row.astype(F32), (8, TILE)), 0.0)
    for place, row in ((IMAGE, image), (GAMMA, gamma), (CROSS, cross)):
        if row is not None:
            tail = tail + jnp.where(sub == place, jnp.broadcast_to(row, (8, TILE)), 0.0)
    part_ref[TILE:PART, :] = tail


def back_first_kernel(
    tiles_hbm, same_ref, other_ref, pack_ref,
    part_ref, share_ref, natural_ref, row_ref, slot_ref, vox_ref, extra_ref, ids_ref,
    picked_ref, index_ref, place_ref, sems,
):
    size = TILE // CHUNKS
    moves = []
    for chunk in range(CHUNKS):
        where = pl.ds(chunk * size, size)
        moves.append(pltpu.make_async_copy(tiles_hbm.at[where], natural_ref.at[where], sems.at[chunk]))
    for move in moves:
        move.start()

    owned = same_ref.shape[0] // CHIPS
    slot, vox = pack_ref[0:1, :], pack_ref[2:3, :]
    target, place = lax.shift_right_logical(slot, 2), slot & (CAP - 1)
    sub, lane = iota((TILE, TILE), 0), iota((TILE, TILE), 1)
    column = jnp.transpose(jnp.broadcast_to(pack_ref[1:2, :].astype(F32), (TILE, TILE)))
    block = jnp.sum(jnp.where(sub == slot, column, 0.0), axis=0, keepdims=True).astype(jnp.int32)
    mine = lax.axis_index("vox") & (CORES - 1)
    other = (target & (CORES - 1)) ^ mine
    index_ref[...] = (other * CHIPS + lax.shift_right_logical(target, 1)) * owned + block
    move = pltpu.make_async_copy(index_ref, place_ref, sems.at[CHUNKS])
    move.start()

    row_ref[...] = target * PAD + place
    slot_ref[...] = slot
    vox_ref[...] = vox
    ids_ref[...] = jnp.broadcast_to(vox.astype(F32), (8, TILE))
    write_tail(part_ref, vox, None, None, None)
    values = jnp.where((sub & (CAP - 1)) == lane, column, 0.0).astype(BF16)
    sub, lane = iota((SENT, TILE), 0), iota((SENT, TILE), 1)
    hit = ((sub & (PAD - 1)) == MAP) & (lax.shift_right_logical(lane, 2) == lax.shift_right_logical(sub, 3))
    choice = jnp.where(hit, 1.0, 0.0).astype(BF16)
    extra_ref[...] = jnp.dot(choice, values, preferred_element_type=F32)

    move.wait()
    half = same_ref.shape[0]
    for tile in range(TILE):
        index = place_ref[0, tile]
        here = index < half
        row = jnp.where(here, index, index - half)
        picked_ref[tile : tile + 1, :] = jnp.where(here, same_ref[pl.ds(row, 1), :], other_ref[pl.ds(row, 1), :])
    weight = jnp.transpose(picked_ref[...])
    for group in range(TILE // 8):
        if group * 8 % size == 0:
            moves[group * 8 // size].wait()
        rows = []
        for tile in range(group * 8, group * 8 + 8):
            rows.append(jnp.sum(natural_ref[tile] * weight[:, tile : tile + 1], axis=0, keepdims=True))
        part_ref[group * 8 : group * 8 + 8, :] = jnp.concatenate(rows, axis=0)
    share_ref[...] = jnp.transpose(part_ref[0:TILE, :])


def back_share(received_ref, tiles_ref, row_ref, vox_ref, part_ref, weight_ref):
    received = received_ref[...]
    weight_ref[...] = select_columns(jnp.transpose(received), one_hot(SENT, row_ref[...]))
    heads = jnp.sum(received.reshape(N_VOX, PAD, TILE), axis=0)
    share = back_tiles(tiles_ref, weight_ref)
    part_ref[0:TILE, :] = jnp.transpose(share)
    write_tail(part_ref, vox_ref[...], *(heads[row : row + 1, :] for row in (NORM, LOCAL, OTHER)))
    return share


def back_kernel(received_ref, tiles_ref, row_ref, vox_ref, part_ref, share_ref, weight_ref):
    share_ref[...] = back_share(received_ref, tiles_ref, row_ref, vox_ref, part_ref, weight_ref)


def back_last_kernel(received_ref, tiles_ref, row_ref, vox_ref, part_ref, weight_ref):
    back_share(received_ref, tiles_ref, row_ref, vox_ref, part_ref, weight_ref)


def quad_sum(own_ref, one_ref, two_ref, three_ref):
    def spread(ref):
        where = ref[TILE + IDS : TILE + IDS + 1, :].astype(jnp.int32)
        return select_rows(one_hot(VT_DEV, where), ref[0:TILE, :])

    field = (spread(own_ref) + spread(one_ref)) + (spread(two_ref) + spread(three_ref))
    tail = slice(TILE, PART)
    return field, (own_ref[tail, :] + one_ref[tail, :]) + (two_ref[tail, :] + three_ref[tail, :])


def read_tiles(field, tail, own_ref, ids_ref, mine_ref, send_ref):
    here = one_hot(VT_DEV, own_ref[TILE + IDS : TILE + IDS + 1, :].astype(jnp.int32))
    there = one_hot(VT_DEV, ids_ref[0:1, :].astype(jnp.int32))
    both = select_columns(jnp.transpose(field), jnp.concatenate([here, there], axis=1))
    mine_ref[...] = both[:, 0:TILE]
    send_ref[0:TILE, :] = both[:, TILE : 2 * TILE]
    send_ref[TILE:PART, :] = tail


def quad_first_kernel(own_ref, one_ref, two_ref, three_ref, ids_ref, near_ref, mine_ref, send_ref):
    field, tail = quad_sum(own_ref, one_ref, two_ref, three_ref)
    read_tiles(field, tail, own_ref, ids_ref, mine_ref, send_ref)
    near_ref[...] = field


def quad_kernel(own_ref, one_ref, two_ref, three_ref, ids_ref, before_ref, near_ref, mine_ref, send_ref):
    field, tail = quad_sum(own_ref, one_ref, two_ref, three_ref)
    read_tiles(field, tail, own_ref, ids_ref, mine_ref, send_ref)
    near_ref[0:VT_DEV, :] = before_ref[...]
    near_ref[VT_DEV:, :] = field


def quad_last_kernel(own_ref, one_ref, two_ref, three_ref, near_ref):
    field, tail = quad_sum(own_ref, one_ref, two_ref, three_ref)
    near_ref[0:VT_DEV, :] = field
    near_ref[VT_DEV:SUM, :] = tail


def forward_tiles(values, share, tiles_ref, gamma_ref, sums_ref):
    def step(index, unused):
        for inner in range(8):
            ray = index * 8 + inner
            product = tiles_ref[ray] * values
            sums_ref[pl.ds(pl.multiple_of(ray * 8, 8), 8), :] = jnp.sum(product.reshape(TILE // 8, 8, TILE), axis=0)
        return unused

    lax.fori_loop(0, TILE // 8, step, 0)
    gamma_ref[...] = jnp.broadcast_to(jnp.sum(values * share, axis=0, keepdims=True), (8, TILE))
    rays = sums_ref[pl.ds(0, TILE, stride=8), :]
    for inner in range(1, 8):
        rays = rays + sums_ref[pl.ds(inner, TILE, stride=8), :]
    return jnp.transpose(rays)


def forward_first_kernel(
    mine_ref, far_ref, share_ref, tiles_ref, row_ref, extra_ref, payload_ref, values_ref, gamma_ref, sums_ref
):
    values = mine_ref[...] + far_ref[0:TILE, :]
    values_ref[...] = values
    rays = forward_tiles(values, share_ref[...], tiles_ref, gamma_ref, sums_ref)
    payload_ref[...] = select_rows(one_hot(SENT, row_ref[...]), rays) + extra_ref[...]


def lane_sum(tail, place):
    return jnp.sum(tail[place : place + 1, :], axis=1, keepdims=True)


def forward_kernel(
    mine_ref, send_ref, far_ref, share_ref, values0_ref, share0_ref, tiles_ref, slot_ref,
    payload_ref, scalars_ref, gamma_ref, sums_ref,
):
    tail = send_ref[TILE:PART, :] + far_ref[TILE:PART, :]
    gamma, square = lane_sum(tail, GAMMA), lane_sum(tail, IMAGE)
    step = gamma / square
    sub = iota((8, TILE), 0)
    scalars_ref[...] = jnp.where(sub == 0, gamma, jnp.where(sub == 1, square, step))
    values = values0_ref[...] - step * (mine_ref[...] + far_ref[0:TILE, :])
    share = share0_ref[...] - step * share_ref[...]
    rays = forward_tiles(values, share, tiles_ref, gamma_ref, sums_ref)
    payload_ref[...] = select_rows(one_hot(TILE, slot_ref[...]), rays)


def back_message(choice, image, rows):
    place = iota((SENT, TILE), 0) & (PAD - 1)
    head = jnp.zeros((SENT, TILE), F32)
    for where, row in rows:
        head = jnp.where(place == where, row, head)
    return select_rows(choice, image) + head


def owner_first_kernel(received_ref, gamma_ref, payload_ref, image_ref, choice_ref, compact_ref):
    received = received_ref[...]
    blocks = received.reshape(N_VOX, PAD, TILE)
    head = jnp.broadcast_to(blocks[:, MAP : MAP + 1, :], (N_VOX, PAD, TILE)).reshape(SENT, TILE)
    place, lane = iota((SENT, TILE), 0) & (PAD - 1), iota((SENT, TILE), 1)
    column = jnp.sum(jnp.where((lane == place) & (place < CAP), head, 0.0), axis=1, keepdims=True)
    hit = (column.astype(jnp.int32) == lane) & (place < CAP)
    choice = jnp.where(hit, 1.0, 0.0)
    image = select_rows(jnp.transpose(choice).astype(BF16), received)
    owned = image_ref.shape[0]
    lower = image[0:owned, :]
    image_ref[...] = lower
    square = jnp.sum(lower * lower, axis=0, keepdims=True)
    payload_ref[...] = back_message(choice.astype(BF16), image, ((NORM, square), (LOCAL, gamma_ref[0:1, :])))
    choice_ref[...] = choice
    compact_ref[...] = jnp.transpose(choice.reshape(N_VOX, PAD, TILE)[:, 0:CAP, :].reshape(TILE, TILE))


def owner_kernel(received_ref, gamma_ref, image0_ref, choice_ref, compact_ref, payload_ref, image_ref):
    image = select_rows(compact_ref[...].astype(BF16), received_ref[...])
    owned = image_ref.shape[0]
    lower = image[0:owned, :]
    image_ref[...] = lower
    square = jnp.sum(lower * lower, axis=0, keepdims=True)
    cross = jnp.sum(lower * image0_ref[...], axis=0, keepdims=True)
    rows = ((NORM, square), (LOCAL, gamma_ref[0:1, :]), (OTHER, cross))
    payload_ref[...] = back_message(choice_ref[...].astype(BF16), image, rows)


def last_kernel(
    near_ref, far_ref, inner_near_ref, inner_far_ref, scalars_ref, image0_ref, image1_ref, ray_ref,
    solution_ref, residual_ref, normal_ref,
):
    tail = near_ref[VT_DEV:SUM, :] + far_ref[VT_DEV:SUM, :]
    gamma0, square0, step0 = scalars_ref[0:1, :], scalars_ref[1:2, :], scalars_ref[2:3, :]
    gamma1 = lane_sum(tail, GAMMA)
    ratio = gamma1 / gamma0
    square1 = lane_sum(tail, IMAGE) + 2.0 * ratio * lane_sum(tail, CROSS) + ratio * ratio * square0
    step1 = gamma1 / square1
    normal0 = inner_near_ref[0:VT_DEV, :] + inner_far_ref[0:VT_DEV, :]
    change0 = inner_near_ref[VT_DEV:, :] + inner_far_ref[VT_DEV:, :]
    normal1 = normal0 - step0 * change0
    change1 = near_ref[0:VT_DEV, :] + far_ref[0:VT_DEV, :] + ratio * change0
    solution_ref[...] = step0 * normal0 + step1 * (normal1 + ratio * normal0)
    normal_ref[...] = normal1 - step1 * change1
    image0 = image0_ref[...]
    residual_ref[...] = ray_ref[...] - step0 * image0 - step1 * (image1_ref[...] + ratio * image0)


def call(kernel, outs, scratch, args, hbm=0, cost=None, limit=24):
    vmem = pl.BlockSpec(memory_space=pltpu.VMEM)
    specs = [pl.BlockSpec(memory_space=pl.ANY)] * hbm
    outs = [out if isinstance(out, jax.ShapeDtypeStruct) else jax.ShapeDtypeStruct(out, F32) for out in outs]
    return pl.pallas_call(
        kernel,
        out_shape=outs,
        in_specs=specs + [vmem] * (len(args) - hbm),
        out_specs=[vmem] * len(outs),
        scratch_shapes=[pltpu.VMEM(shape, F32) if isinstance(shape, tuple) else shape for shape in scratch],
        cost_estimate=cost,
        compiler_params=pltpu.CompilerParams(vmem_limit_bytes=limit * 1024 * 1024),
    )(*args)


def local(tile_values, tile_vox, tile_slot, slot_block, ray_data):
    owned = ray_data.shape[0]
    block = (TILE, TILE)
    sent = (SENT, TILE)
    field = (VT_DEV, TILE)
    scalar = (8, TILE)
    part = (PART, TILE)
    sums = (TILE * 8, TILE)
    rays = (owned, TILE)
    indices = jax.ShapeDtypeStruct((1, TILE), jnp.int32)

    def over_vox(array):
        return lax.all_to_all(array, "vox", 0, 0, tiled=True)

    def across(array, distance):
        return lax.ppermute(array, "row", [(index, index ^ distance) for index in range(N_ROW)])

    def quad(own):
        return (own, *(across(own, distance) for distance in (1, 2, 3)))

    (copies,) = call(copies_kernel, [(CHIPS * owned, TILE)], [], (ray_data,))
    chips = [[chip * CORES + core for chip in range(CHIPS)] for core in range(CORES)]
    same = lax.all_to_all(copies, "vox", 0, 0, tiled=True, axis_index_groups=chips)
    same, tile_vox, tile_slot, slot_block = lax.optimization_barrier((same, tile_vox, tile_slot, slot_block))
    other = lax.ppermute(same, "vox", [(device, device ^ 1) for device in range(N_VOX)])
    (pack,) = call(
        pack_kernel,
        [jax.ShapeDtypeStruct(scalar, jnp.int32)],
        [],
        (tile_slot.reshape(1, TILE), slot_block, tile_vox.reshape(1, TILE)),
    )
    own, share0, natural, slot_row, slot, vox_row, extra, ids = call(
        back_first_kernel,
        [part, block, (TILE, TILE, TILE), indices, indices, indices, sent, scalar],
        [
            block,
            pltpu.VMEM((1, TILE), jnp.int32),
            pltpu.SMEM((1, TILE), jnp.int32),
            pltpu.SemaphoreType.DMA((CHUNKS + 1,)),
        ],
        (tile_values, same, other, pack),
        hbm=1,
        limit=42,
    )
    ids = across(ids, 6)
    near, mine, send = call(quad_first_kernel, [field, block, part], [], (*quad(own), ids))
    send, natural = lax.optimization_barrier((send, natural))
    far = across(send, 6)
    (tiles,) = call(
        relay_kernel,
        [(TILE, TILE, TILE)],
        [],
        (natural,),
        cost=pl.CostEstimate(flops=0, bytes_accessed=2**24, transcendentals=0),
    )
    payload, values0, gamma = call(
        forward_first_kernel, [sent, block, scalar], [sums], (mine, far, share0, tiles, slot_row, extra)
    )
    payload, image0, choice, compact = call(
        owner_first_kernel, [sent, rays, sent, block], [], (over_vox(payload), gamma)
    )
    own, share = call(back_kernel, [part, block], [block], (over_vox(payload), tiles, slot_row, vox_row))
    near, mine, send = call(
        quad_kernel, [(2 * VT_DEV, TILE), block, part], [], (*quad(own), ids, near)
    )
    far, near = lax.optimization_barrier((across(send, 6), near))
    inner_far = across(near, 6)
    payload, scalars, gamma = call(
        forward_kernel,
        [block, scalar, scalar],
        [sums],
        (mine, send, far, share, values0, share0, tiles, slot),
    )
    received, inner_far = lax.optimization_barrier((over_vox(payload), inner_far))
    payload, image1 = call(owner_kernel, [sent, rays], [], (received, gamma, image0, choice, compact))
    (own,) = call(back_last_kernel, [part], [block], (over_vox(payload), tiles, slot_row, vox_row))
    (last,) = call(quad_last_kernel, [(SUM, TILE)], [], quad(own))
    return tuple(
        call(
            last_kernel,
            [field, rays, field],
            [],
            (last, across(last, 6), near, inner_far, scalars, image0, image1, ray_data),
        )
    )


def solution(mesh):
    return jax.shard_map(
        local,
        mesh=mesh,
        in_specs=(
            P(("vox", "row"), None, None),
            P(("vox", "row")),
            P(("vox", "row")),
            P(("vox", "row"), None),
            P(("vox", "row"), None),
        ),
        out_specs=(P("vox", None), P(("vox", "row"), None), P("vox", None)),
        check_vma=False,
    )
```

```python
import functools

import jax
import jax.numpy as jnp
from jax import lax
from jax.experimental import pallas as pl
from jax.experimental.pallas import tpu as pltpu
from jax.sharding import PartitionSpec as P

TILE = 128
VT_DEV = 256
CAP = 4
N_VOX = 32
N_ROW = 8
CORES = 2
HALF = TILE // 2
CHIPS = N_VOX // CORES
CHUNKS = 8
PAD = 8
MAP = CAP
NORM, LOCAL, OTHER = CAP, CAP + 1, CAP + 2
SENT = N_VOX * PAD
PART = TILE + 8
SUM = VT_DEV + 8
IDS, IMAGE, GAMMA, CROSS = 0, 1, 2, 3

F32 = jnp.float32
BF16 = jnp.bfloat16


def iota(shape, dim):
    return lax.broadcasted_iota(jnp.int32, shape, dim)


def three_terms(values):
    high = values.astype(BF16)
    rest = values - high.astype(F32)
    middle = rest.astype(BF16)
    return high, middle, (rest - middle.astype(F32)).astype(BF16)


def select_rows(choice, values):
    high, middle, low = three_terms(values)
    small = jnp.dot(choice, jnp.concatenate([middle, low], axis=1), preferred_element_type=F32)
    small = small[:, TILE:] + small[:, 0:TILE]
    return small + jnp.dot(choice, high, preferred_element_type=F32)


def select_columns(values, choice):
    rows = values.shape[0]
    terms = jnp.dot(jnp.concatenate(three_terms(values), axis=0), choice, preferred_element_type=F32)
    return (terms[2 * rows :, :] + terms[rows : 2 * rows, :]) + terms[0:rows, :]


def one_hot(rows, index):
    return jnp.where(iota((rows, TILE), 0) == index, 1.0, 0.0).astype(BF16)


def copies_kernel(ray_ref, copies_ref):
    owned = ray_ref.shape[0]
    rays = ray_ref[...]
    for chip in range(CHIPS):
        copies_ref[chip * owned : (chip + 1) * owned, :] = rays


def pack_kernel(slot_ref, map_ref, vox_ref, pack_ref):
    pack_ref[...] = jnp.zeros_like(pack_ref)
    pack_ref[0:1, :] = slot_ref[...]
    pack_ref[1:2, :] = map_ref[...]
    pack_ref[2:3, :] = vox_ref[...]


def relay_kernel(natural_ref, tiles_ref, *, first):
    def step(index, unused):
        block = natural_ref[:, pl.ds(pl.multiple_of(first + index * 8, 8), 8), :]
        block = jnp.swapaxes(block, 0, 1)
        for inner in range(8):
            tiles_ref[index * 8 + inner] = jnp.transpose(block[inner])
        return unused

    lax.fori_loop(0, HALF // 8, step, 0)


def back_tiles(low_ref, high_ref, weight_ref):
    total = jnp.zeros((TILE, TILE), F32)
    for first, tiles_ref in ((0, low_ref), (HALF, high_ref)):

        def step(index, total):
            for inner in range(8):
                ray = index * 8 + inner
                total = total + tiles_ref[ray] * weight_ref[pl.ds(first + ray, 1), :]
            return total

        total = lax.fori_loop(0, HALF // 8, step, total)
    return total


def write_tail(part_ref, vox_row, image, gamma, cross):
    sub = iota((8, TILE), 0)
    tail = jnp.where(sub == IDS, jnp.broadcast_to(vox_row.astype(F32), (8, TILE)), 0.0)
    for place, row in ((IMAGE, image), (GAMMA, gamma), (CROSS, cross)):
        if row is not None:
            tail = tail + jnp.where(sub == place, jnp.broadcast_to(row, (8, TILE)), 0.0)
    part_ref[TILE:PART, :] = tail


def back_first_kernel(
    tiles_hbm, same_ref, other_ref, pack_ref,
    part_ref, share_ref, natural_ref, row_ref, slot_ref, vox_ref, extra_ref, ids_ref,
    picked_ref, index_ref, place_ref, sems,
):
    size = TILE // CHUNKS
    moves = []
    for chunk in range(CHUNKS):
        where = pl.ds(chunk * size, size)
        moves.append(pltpu.make_async_copy(tiles_hbm.at[where], natural_ref.at[where], sems.at[chunk]))
    for move in moves:
        move.start()

    owned = same_ref.shape[0] // CHIPS
    slot, vox = pack_ref[0:1, :], pack_ref[2:3, :]
    target, place = lax.shift_right_logical(slot, 2), slot & (CAP - 1)
    sub, lane = iota((TILE, TILE), 0), iota((TILE, TILE), 1)
    column = jnp.transpose(jnp.broadcast_to(pack_ref[1:2, :].astype(F32), (TILE, TILE)))
    block = jnp.sum(jnp.where(sub == slot, column, 0.0), axis=0, keepdims=True).astype(jnp.int32)
    mine = lax.axis_index("vox") & (CORES - 1)
    other = (target & (CORES - 1)) ^ mine
    index_ref[...] = (other * CHIPS + lax.shift_right_logical(target, 1)) * owned + block
    move = pltpu.make_async_copy(index_ref, place_ref, sems.at[CHUNKS])
    move.start()

    row_ref[...] = target * PAD + place
    slot_ref[...] = slot
    vox_ref[...] = vox
    ids_ref[...] = jnp.broadcast_to(vox.astype(F32), (8, TILE))
    write_tail(part_ref, vox, None, None, None)
    values = jnp.where((sub & (CAP - 1)) == lane, column, 0.0).astype(BF16)
    sub, lane = iota((SENT, TILE), 0), iota((SENT, TILE), 1)
    hit = ((sub & (PAD - 1)) == MAP) & (lax.shift_right_logical(lane, 2) == lax.shift_right_logical(sub, 3))
    choice = jnp.where(hit, 1.0, 0.0).astype(BF16)
    extra_ref[...] = jnp.dot(choice, values, preferred_element_type=F32)

    move.wait()
    half = same_ref.shape[0]
    for tile in range(TILE):
        index = place_ref[0, tile]
        here = index < half
        row = index & (half - 1)
        picked_ref[tile : tile + 1, :] = jnp.where(here, same_ref[pl.ds(row, 1), :], other_ref[pl.ds(row, 1), :])
    weight = jnp.transpose(picked_ref[...])
    for group in range(TILE // 8):
        if group * 8 % size == 0:
            moves[group * 8 // size].wait()
        rows = []
        for tile in range(group * 8, group * 8 + 8):
            rows.append(jnp.sum(natural_ref[tile] * weight[:, tile : tile + 1], axis=0, keepdims=True))
        part_ref[group * 8 : group * 8 + 8, :] = jnp.concatenate(rows, axis=0)
    share_ref[...] = jnp.transpose(part_ref[0:TILE, :])


def back_share(received_ref, low_ref, high_ref, row_ref, vox_ref, part_ref, weight_ref):
    received = received_ref[...]
    weight_ref[...] = select_columns(jnp.transpose(received), one_hot(SENT, row_ref[...]))
    heads = jnp.sum(received.reshape(N_VOX, PAD, TILE), axis=0)
    share = back_tiles(low_ref, high_ref, weight_ref)
    part_ref[0:TILE, :] = jnp.transpose(share)
    write_tail(part_ref, vox_ref[...], *(heads[row : row + 1, :] for row in (NORM, LOCAL, OTHER)))
    return share


def back_kernel(received_ref, low_ref, high_ref, row_ref, vox_ref, part_ref, share_ref, weight_ref):
    share_ref[...] = back_share(received_ref, low_ref, high_ref, row_ref, vox_ref, part_ref, weight_ref)


def back_last_kernel(received_ref, low_ref, high_ref, row_ref, vox_ref, part_ref, weight_ref):
    back_share(received_ref, low_ref, high_ref, row_ref, vox_ref, part_ref, weight_ref)


def quad_sum(own_ref, one_ref, two_ref, three_ref):
    def spread(ref):
        where = ref[TILE + IDS : TILE + IDS + 1, :].astype(jnp.int32)
        return select_rows(one_hot(VT_DEV, where), ref[0:TILE, :])

    field = (spread(own_ref) + spread(one_ref)) + (spread(two_ref) + spread(three_ref))
    tail = slice(TILE, PART)
    return field, (own_ref[tail, :] + one_ref[tail, :]) + (two_ref[tail, :] + three_ref[tail, :])


def read_tiles(field, tail, own_ref, ids_ref, mine_ref, send_ref):
    here = one_hot(VT_DEV, own_ref[TILE + IDS : TILE + IDS + 1, :].astype(jnp.int32))
    there = one_hot(VT_DEV, ids_ref[0:1, :].astype(jnp.int32))
    both = select_columns(jnp.transpose(field), jnp.concatenate([here, there], axis=1))
    mine_ref[...] = both[:, 0:TILE]
    send_ref[0:TILE, :] = both[:, TILE : 2 * TILE]
    send_ref[TILE:PART, :] = tail


def quad_first_kernel(own_ref, one_ref, two_ref, three_ref, ids_ref, near_ref, mine_ref, send_ref):
    field, tail = quad_sum(own_ref, one_ref, two_ref, three_ref)
    read_tiles(field, tail, own_ref, ids_ref, mine_ref, send_ref)
    near_ref[...] = field


def quad_kernel(own_ref, one_ref, two_ref, three_ref, ids_ref, before_ref, near_ref, mine_ref, send_ref):
    field, tail = quad_sum(own_ref, one_ref, two_ref, three_ref)
    read_tiles(field, tail, own_ref, ids_ref, mine_ref, send_ref)
    near_ref[0:VT_DEV, :] = before_ref[...]
    near_ref[VT_DEV:, :] = field


def quad_last_kernel(own_ref, one_ref, two_ref, three_ref, near_ref):
    field, tail = quad_sum(own_ref, one_ref, two_ref, three_ref)
    near_ref[0:VT_DEV, :] = field
    near_ref[VT_DEV:SUM, :] = tail


def forward_tiles(values, share, low_ref, high_ref, gamma_ref, sums_ref):
    for first, tiles_ref in ((0, low_ref), (HALF, high_ref)):

        def step(index, unused):
            for inner in range(8):
                ray = index * 8 + inner
                product = tiles_ref[ray] * values
                row = pl.multiple_of((first + ray) * 8, 8)
                sums_ref[pl.ds(row, 8), :] = jnp.sum(product.reshape(TILE // 8, 8, TILE), axis=0)
            return unused

        lax.fori_loop(0, HALF // 8, step, 0)
    gamma_ref[...] = jnp.broadcast_to(jnp.sum(values * share, axis=0, keepdims=True), (8, TILE))
    rays = sums_ref[pl.ds(0, TILE, stride=8), :]
    for inner in range(1, 8):
        rays = rays + sums_ref[pl.ds(inner, TILE, stride=8), :]
    return jnp.transpose(rays)


def forward_first_kernel(
    mine_ref, far_ref, share_ref, low_ref, high_ref, row_ref, extra_ref, payload_ref, values_ref, gamma_ref, sums_ref
):
    values = mine_ref[...] + far_ref[0:TILE, :]
    values_ref[...] = values
    rays = forward_tiles(values, share_ref[...], low_ref, high_ref, gamma_ref, sums_ref)
    payload_ref[...] = select_rows(one_hot(SENT, row_ref[...]), rays) + extra_ref[...]


def lane_sum(tail, place):
    return jnp.sum(tail[place : place + 1, :], axis=1, keepdims=True)


def forward_kernel(
    mine_ref, send_ref, far_ref, share_ref, values0_ref, share0_ref, low_ref, high_ref, slot_ref,
    payload_ref, scalars_ref, gamma_ref, sums_ref,
):
    tail = send_ref[TILE:PART, :] + far_ref[TILE:PART, :]
    gamma, square = lane_sum(tail, GAMMA), lane_sum(tail, IMAGE)
    step = gamma / square
    sub = iota((8, TILE), 0)
    scalars_ref[...] = jnp.where(sub == 0, gamma, jnp.where(sub == 1, square, step))
    values = values0_ref[...] - step * (mine_ref[...] + far_ref[0:TILE, :])
    share = share0_ref[...] - step * share_ref[...]
    rays = forward_tiles(values, share, low_ref, high_ref, gamma_ref, sums_ref)
    payload_ref[...] = select_rows(one_hot(TILE, slot_ref[...]), rays)


def back_message(choice, image, rows):
    place = iota((SENT, TILE), 0) & (PAD - 1)
    head = jnp.zeros((SENT, TILE), F32)
    for where, row in rows:
        head = jnp.where(place == where, row, head)
    return select_rows(choice, image) + head


def owner_first_kernel(received_ref, gamma_ref, payload_ref, image_ref, choice_ref, compact_ref):
    received = received_ref[...]
    blocks = received.reshape(N_VOX, PAD, TILE)
    head = jnp.broadcast_to(blocks[:, MAP : MAP + 1, :], (N_VOX, PAD, TILE)).reshape(SENT, TILE)
    place, lane = iota((SENT, TILE), 0) & (PAD - 1), iota((SENT, TILE), 1)
    column = jnp.sum(jnp.where((lane == place) & (place < CAP), head, 0.0), axis=1, keepdims=True)
    hit = (column.astype(jnp.int32) == lane) & (place < CAP)
    choice = jnp.where(hit, 1.0, 0.0)
    image = select_rows(jnp.transpose(choice).astype(BF16), received)
    owned = image_ref.shape[0]
    lower = image[0:owned, :]
    image_ref[...] = lower
    square = jnp.sum(lower * lower, axis=0, keepdims=True)
    payload_ref[...] = back_message(choice.astype(BF16), image, ((NORM, square), (LOCAL, gamma_ref[0:1, :])))
    choice_ref[...] = choice
    compact_ref[...] = jnp.transpose(choice.reshape(N_VOX, PAD, TILE)[:, 0:CAP, :].reshape(TILE, TILE))


def owner_kernel(received_ref, gamma_ref, image0_ref, choice_ref, compact_ref, payload_ref, image_ref):
    image = select_rows(compact_ref[...].astype(BF16), received_ref[...])
    owned = image_ref.shape[0]
    lower = image[0:owned, :]
    image_ref[...] = lower
    square = jnp.sum(lower * lower, axis=0, keepdims=True)
    cross = jnp.sum(lower * image0_ref[...], axis=0, keepdims=True)
    rows = ((NORM, square), (LOCAL, gamma_ref[0:1, :]), (OTHER, cross))
    payload_ref[...] = back_message(choice_ref[...].astype(BF16), image, rows)


def last_kernel(
    near_ref, far_ref, inner_near_ref, inner_far_ref, scalars_ref, image0_ref, image1_ref, ray_ref,
    solution_ref, residual_ref, normal_ref,
):
    tail = near_ref[VT_DEV:SUM, :] + far_ref[VT_DEV:SUM, :]
    gamma0, square0, step0 = scalars_ref[0:1, :], scalars_ref[1:2, :], scalars_ref[2:3, :]
    gamma1 = lane_sum(tail, GAMMA)
    ratio = gamma1 / gamma0
    square1 = lane_sum(tail, IMAGE) + 2.0 * ratio * lane_sum(tail, CROSS) + ratio * ratio * square0
    step1 = gamma1 / square1
    normal0 = inner_near_ref[0:VT_DEV, :] + inner_far_ref[0:VT_DEV, :]
    change0 = inner_near_ref[VT_DEV:, :] + inner_far_ref[VT_DEV:, :]
    normal1 = normal0 - step0 * change0
    change1 = near_ref[0:VT_DEV, :] + far_ref[0:VT_DEV, :] + ratio * change0
    solution_ref[...] = step0 * normal0 + step1 * (normal1 + ratio * normal0)
    normal_ref[...] = normal1 - step1 * change1
    image0 = image0_ref[...]
    residual_ref[...] = ray_ref[...] - step0 * image0 - step1 * (image1_ref[...] + ratio * image0)


def call(kernel, outs, scratch, args, hbm=0, cost=None, limit=24):
    vmem = pl.BlockSpec(memory_space=pltpu.VMEM)
    specs = [pl.BlockSpec(memory_space=pl.ANY)] * hbm
    outs = [out if isinstance(out, jax.ShapeDtypeStruct) else jax.ShapeDtypeStruct(out, F32) for out in outs]
    return pl.pallas_call(
        kernel,
        out_shape=outs,
        in_specs=specs + [vmem] * (len(args) - hbm),
        out_specs=[vmem] * len(outs),
        scratch_shapes=[pltpu.VMEM(shape, F32) if isinstance(shape, tuple) else shape for shape in scratch],
        cost_estimate=cost,
        compiler_params=pltpu.CompilerParams(vmem_limit_bytes=limit * 1024 * 1024),
    )(*args)


def local(tile_values, tile_vox, tile_slot, slot_block, ray_data):
    owned = ray_data.shape[0]
    block = (TILE, TILE)
    sent = (SENT, TILE)
    field = (VT_DEV, TILE)
    scalar = (8, TILE)
    part = (PART, TILE)
    sums = (TILE * 8, TILE)
    rays = (owned, TILE)
    indices = jax.ShapeDtypeStruct((1, TILE), jnp.int32)

    def over_vox(array):
        return lax.all_to_all(array, "vox", 0, 0, tiled=True)

    def across(array, distance):
        return lax.ppermute(array, "row", [(index, index ^ distance) for index in range(N_ROW)])

    def quad(own):
        return (own, *(across(own, distance) for distance in (1, 2, 3)))

    (copies,) = call(copies_kernel, [(CHIPS * owned, TILE)], [], (ray_data,))
    chips = [[chip * CORES + core for chip in range(CHIPS)] for core in range(CORES)]
    same = lax.all_to_all(copies, "vox", 0, 0, tiled=True, axis_index_groups=chips)
    same, tile_vox, tile_slot, slot_block = lax.optimization_barrier((same, tile_vox, tile_slot, slot_block))
    other = lax.ppermute(same, "vox", [(device, device ^ 1) for device in range(N_VOX)])
    (pack,) = call(
        pack_kernel,
        [jax.ShapeDtypeStruct(scalar, jnp.int32)],
        [],
        (tile_slot.reshape(1, TILE), slot_block, tile_vox.reshape(1, TILE)),
    )
    own, share0, natural, slot_row, slot, vox_row, extra, ids = call(
        back_first_kernel,
        [part, block, (TILE, TILE, TILE), indices, indices, indices, sent, scalar],
        [
            block,
            pltpu.VMEM((1, TILE), jnp.int32),
            pltpu.SMEM((1, TILE), jnp.int32),
            pltpu.SemaphoreType.DMA((CHUNKS + 1,)),
        ],
        (tile_values, same, other, pack),
        hbm=1,
        limit=42,
    )
    ids = across(ids, 6)
    def relay(natural, first):
        return call(
            functools.partial(relay_kernel, first=first),
            [(HALF, TILE, TILE)],
            [],
            (natural,),
            cost=pl.CostEstimate(flops=0, bytes_accessed=2**23, transcendentals=0),
        )[0]

    messages = quad(own)
    low = relay(natural, 0)
    messages, ids, low = lax.optimization_barrier((messages, ids, low))
    near, mine, send = call(quad_first_kernel, [field, block, part], [], (*messages, ids))
    send, natural = lax.optimization_barrier((send, natural))
    far = across(send, 6)
    high = relay(natural, HALF)
    payload, values0, gamma = call(
        forward_first_kernel, [sent, block, scalar], [sums], (mine, far, share0, low, high, slot_row, extra)
    )
    payload, image0, choice, compact = call(
        owner_first_kernel, [sent, rays, sent, block], [], (over_vox(payload), gamma)
    )
    own, share = call(back_kernel, [part, block], [block], (over_vox(payload), low, high, slot_row, vox_row))
    near, mine, send = call(
        quad_kernel, [(2 * VT_DEV, TILE), block, part], [], (*quad(own), ids, near)
    )
    far, near = lax.optimization_barrier((across(send, 6), near))
    inner_far = across(near, 6)
    payload, scalars, gamma = call(
        forward_kernel,
        [block, scalar, scalar],
        [sums],
        (mine, send, far, share, values0, share0, low, high, slot),
    )
    received, inner_far = lax.optimization_barrier((over_vox(payload), inner_far))
    payload, image1 = call(owner_kernel, [sent, rays], [], (received, gamma, image0, choice, compact))
    (own,) = call(back_last_kernel, [part], [block], (over_vox(payload), low, high, slot_row, vox_row))
    (last,) = call(quad_last_kernel, [(SUM, TILE)], [], quad(own))
    return tuple(
        call(
            last_kernel,
            [field, rays, field],
            [],
            (last, across(last, 6), near, inner_far, scalars, image0, image1, ray_data),
        )
    )


def solution(mesh):
    return jax.shard_map(
        local,
        mesh=mesh,
        in_specs=(
            P(("vox", "row"), None, None),
            P(("vox", "row")),
            P(("vox", "row")),
            P(("vox", "row"), None),
            P(("vox", "row"), None),
        ),
        out_specs=(P("vox", None), P(("vox", "row"), None), P("vox", None)),
        check_vma=False,
    )
```

```python
import functools

import jax
import jax.numpy as jnp
from jax import lax
from jax.experimental import pallas as pl
from jax.experimental.pallas import tpu as pltpu
from jax.sharding import PartitionSpec as P

TILE = 128
VT_DEV = 256
CAP = 4
N_VOX = 32
N_ROW = 8
CORES = 2
HALF = TILE // 2
CHIPS = N_VOX // CORES
CHUNKS = 8
PAD = 8
MAP = CAP
NORM, LOCAL, OTHER = CAP, CAP + 1, CAP + 2
SENT = N_VOX * PAD
PART = TILE + 8
SUM = VT_DEV + 8
IDS, IMAGE, GAMMA, CROSS = 0, 1, 2, 3

F32 = jnp.float32
BF16 = jnp.bfloat16


def iota(shape, dim):
    return lax.broadcasted_iota(jnp.int32, shape, dim)


def three_terms(values):
    high = values.astype(BF16)
    rest = values - high.astype(F32)
    middle = rest.astype(BF16)
    return high, middle, (rest - middle.astype(F32)).astype(BF16)


def select_rows(choice, values):
    high, middle, low = three_terms(values)
    small = jnp.dot(choice, jnp.concatenate([middle, low], axis=1), preferred_element_type=F32)
    small = small[:, TILE:] + small[:, 0:TILE]
    return small + jnp.dot(choice, high, preferred_element_type=F32)


def select_columns(values, choice):
    rows = values.shape[0]
    terms = jnp.dot(jnp.concatenate(three_terms(values), axis=0), choice, preferred_element_type=F32)
    return (terms[2 * rows :, :] + terms[rows : 2 * rows, :]) + terms[0:rows, :]


def one_hot(rows, index):
    return jnp.where(iota((rows, TILE), 0) == index, 1.0, 0.0).astype(BF16)


def copies_kernel(ray_ref, copies_ref):
    owned = ray_ref.shape[0]
    rays = ray_ref[...]
    for chip in range(CHIPS):
        copies_ref[chip * owned : (chip + 1) * owned, :] = rays


def pack_kernel(slot_ref, map_ref, vox_ref, pack_ref):
    pack_ref[...] = jnp.zeros_like(pack_ref)
    pack_ref[0:1, :] = slot_ref[...]
    pack_ref[1:2, :] = map_ref[...]
    pack_ref[2:3, :] = vox_ref[...]


def relay_kernel(natural_ref, tiles_ref, *, first):
    def step(index, unused):
        block = natural_ref[:, pl.ds(pl.multiple_of(first + index * 8, 8), 8), :]
        block = jnp.swapaxes(block, 0, 1)
        for inner in range(8):
            tiles_ref[index * 8 + inner] = jnp.transpose(block[inner])
        return unused

    lax.fori_loop(0, HALF // 8, step, 0)


def back_tiles(low_ref, high_ref, weight_ref):
    total = jnp.zeros((TILE, TILE), F32)
    for first, tiles_ref in ((0, low_ref), (HALF, high_ref)):

        def step(index, total):
            for inner in range(8):
                ray = index * 8 + inner
                total = total + tiles_ref[ray] * weight_ref[pl.ds(first + ray, 1), :]
            return total

        total = lax.fori_loop(0, HALF // 8, step, total)
    return total


def write_tail(part_ref, vox_row, image, gamma, cross):
    sub = iota((8, TILE), 0)
    tail = jnp.where(sub == IDS, jnp.broadcast_to(vox_row.astype(F32), (8, TILE)), 0.0)
    for place, row in ((IMAGE, image), (GAMMA, gamma), (CROSS, cross)):
        if row is not None:
            tail = tail + jnp.where(sub == place, jnp.broadcast_to(row, (8, TILE)), 0.0)
    part_ref[TILE:PART, :] = tail


def back_first_kernel(
    tiles_hbm, same_ref, other_ref, pack_ref,
    part_ref, share_ref, natural_ref, row_ref, slot_ref, vox_ref, extra_ref, ids_ref,
    picked_ref, sums_ref, index_ref, place_ref, sems,
):
    size = TILE // CHUNKS
    moves = []
    for chunk in range(CHUNKS):
        where = pl.ds(chunk * size, size)
        moves.append(pltpu.make_async_copy(tiles_hbm.at[where], natural_ref.at[where], sems.at[chunk]))
    for move in moves:
        move.start()

    owned = same_ref.shape[0] // CHIPS
    slot, vox = pack_ref[0:1, :], pack_ref[2:3, :]
    target, place = lax.shift_right_logical(slot, 2), slot & (CAP - 1)
    sub, lane = iota((TILE, TILE), 0), iota((TILE, TILE), 1)
    column = jnp.transpose(jnp.broadcast_to(pack_ref[1:2, :].astype(F32), (TILE, TILE)))
    block = jnp.sum(jnp.where(sub == slot, column, 0.0), axis=0, keepdims=True).astype(jnp.int32)
    mine = lax.axis_index("vox") & (CORES - 1)
    other = (target & (CORES - 1)) ^ mine
    index_ref[...] = (other * CHIPS + lax.shift_right_logical(target, 1)) * owned + block
    move = pltpu.make_async_copy(index_ref, place_ref, sems.at[CHUNKS])
    move.start()

    row_ref[...] = target * PAD + place
    slot_ref[...] = slot
    vox_ref[...] = vox
    ids_ref[...] = jnp.broadcast_to(vox.astype(F32), (8, TILE))
    write_tail(part_ref, vox, None, None, None)
    values = jnp.where((sub & (CAP - 1)) == lane, column, 0.0).astype(BF16)
    sub, lane = iota((SENT, TILE), 0), iota((SENT, TILE), 1)
    hit = ((sub & (PAD - 1)) == MAP) & (lax.shift_right_logical(lane, 2) == lax.shift_right_logical(sub, 3))
    choice = jnp.where(hit, 1.0, 0.0).astype(BF16)
    extra_ref[...] = jnp.dot(choice, values, preferred_element_type=F32)

    move.wait()
    half = same_ref.shape[0]
    for tile in range(TILE):
        index = place_ref[0, tile]
        here = index < half
        row = index & (half - 1)
        picked_ref[tile : tile + 1, :] = jnp.where(here, same_ref[pl.ds(row, 1), :], other_ref[pl.ds(row, 1), :])
    weight = jnp.transpose(picked_ref[...])
    for group in range(TILE // 8):
        if group * 8 % size == 0:
            moves[group * 8 // size].wait()
        for tile in range(group * 8, group * 8 + 8):
            product = natural_ref[tile] * weight[:, tile : tile + 1]
            sums_ref[tile * 8 : tile * 8 + 8, :] = jnp.sum(product.reshape(TILE // 8, 8, TILE), axis=0)
    share = sums_ref[pl.ds(0, TILE, stride=8), :]
    for inner in range(1, 8):
        share = share + sums_ref[pl.ds(inner, TILE, stride=8), :]
    part_ref[0:TILE, :] = share
    share_ref[...] = jnp.transpose(share)


def back_share(received_ref, low_ref, high_ref, row_ref, vox_ref, part_ref, weight_ref):
    received = received_ref[...]
    weight_ref[...] = select_columns(jnp.transpose(received), one_hot(SENT, row_ref[...]))
    heads = jnp.sum(received.reshape(N_VOX, PAD, TILE), axis=0)
    share = back_tiles(low_ref, high_ref, weight_ref)
    part_ref[0:TILE, :] = jnp.transpose(share)
    write_tail(part_ref, vox_ref[...], *(heads[row : row + 1, :] for row in (NORM, LOCAL, OTHER)))
    return share


def back_kernel(received_ref, low_ref, high_ref, row_ref, vox_ref, part_ref, share_ref, weight_ref):
    share_ref[...] = back_share(received_ref, low_ref, high_ref, row_ref, vox_ref, part_ref, weight_ref)


def back_last_kernel(received_ref, low_ref, high_ref, row_ref, vox_ref, part_ref, weight_ref):
    back_share(received_ref, low_ref, high_ref, row_ref, vox_ref, part_ref, weight_ref)


def spread(ref):
    where = ref[TILE + IDS : TILE + IDS + 1, :].astype(jnp.int32)
    return select_rows(one_hot(VT_DEV, where), ref[0:TILE, :])


def spread_kernel(own_ref, spread_ref):
    spread_ref[...] = spread(own_ref)


def quad_sum(own_ref, spread_ref, one_ref, two_ref, three_ref):
    field = (spread_ref[...] + spread(one_ref)) + (spread(two_ref) + spread(three_ref))
    tail = slice(TILE, PART)
    return field, (own_ref[tail, :] + one_ref[tail, :]) + (two_ref[tail, :] + three_ref[tail, :])


def read_tiles(field, tail, own_ref, ids_ref, mine_ref, send_ref):
    here = one_hot(VT_DEV, own_ref[TILE + IDS : TILE + IDS + 1, :].astype(jnp.int32))
    there = one_hot(VT_DEV, ids_ref[0:1, :].astype(jnp.int32))
    both = select_columns(jnp.transpose(field), jnp.concatenate([here, there], axis=1))
    mine_ref[...] = both[:, 0:TILE]
    send_ref[0:TILE, :] = both[:, TILE : 2 * TILE]
    send_ref[TILE:PART, :] = tail


def quad_first_kernel(own_ref, spread_ref, one_ref, two_ref, three_ref, ids_ref, near_ref, mine_ref, send_ref):
    field, tail = quad_sum(own_ref, spread_ref, one_ref, two_ref, three_ref)
    read_tiles(field, tail, own_ref, ids_ref, mine_ref, send_ref)
    near_ref[...] = field


def quad_kernel(own_ref, spread_ref, one_ref, two_ref, three_ref, ids_ref, before_ref, near_ref, mine_ref, send_ref):
    field, tail = quad_sum(own_ref, spread_ref, one_ref, two_ref, three_ref)
    read_tiles(field, tail, own_ref, ids_ref, mine_ref, send_ref)
    near_ref[0:VT_DEV, :] = before_ref[...]
    near_ref[VT_DEV:, :] = field


def quad_last_kernel(own_ref, spread_ref, one_ref, two_ref, three_ref, near_ref):
    field, tail = quad_sum(own_ref, spread_ref, one_ref, two_ref, three_ref)
    near_ref[0:VT_DEV, :] = field
    near_ref[VT_DEV:SUM, :] = tail


def forward_tiles(values, share, low_ref, high_ref, gamma_ref, sums_ref):
    for first, tiles_ref in ((0, low_ref), (HALF, high_ref)):

        def step(index, unused):
            for inner in range(8):
                ray = index * 8 + inner
                product = tiles_ref[ray] * values
                row = pl.multiple_of((first + ray) * 8, 8)
                sums_ref[pl.ds(row, 8), :] = jnp.sum(product.reshape(TILE // 8, 8, TILE), axis=0)
            return unused

        lax.fori_loop(0, HALF // 8, step, 0)
    gamma_ref[...] = jnp.broadcast_to(jnp.sum(values * share, axis=0, keepdims=True), (8, TILE))
    rays = sums_ref[pl.ds(0, TILE, stride=8), :]
    for inner in range(1, 8):
        rays = rays + sums_ref[pl.ds(inner, TILE, stride=8), :]
    return jnp.transpose(rays)


def forward_first_kernel(
    mine_ref, far_ref, share_ref, low_ref, high_ref, row_ref, extra_ref, payload_ref, values_ref, gamma_ref, sums_ref
):
    values = mine_ref[...] + far_ref[0:TILE, :]
    values_ref[...] = values
    rays = forward_tiles(values, share_ref[...], low_ref, high_ref, gamma_ref, sums_ref)
    payload_ref[...] = select_rows(one_hot(SENT, row_ref[...]), rays) + extra_ref[...]


def lane_sum(tail, place):
    return jnp.sum(tail[place : place + 1, :], axis=1, keepdims=True)


def forward_kernel(
    mine_ref, send_ref, far_ref, share_ref, values0_ref, share0_ref, low_ref, high_ref, slot_ref,
    payload_ref, scalars_ref, gamma_ref, sums_ref,
):
    tail = send_ref[TILE:PART, :] + far_ref[TILE:PART, :]
    gamma, square = lane_sum(tail, GAMMA), lane_sum(tail, IMAGE)
    step = gamma / square
    sub = iota((8, TILE), 0)
    scalars_ref[...] = jnp.where(sub == 0, gamma, jnp.where(sub == 1, square, step))
    values = values0_ref[...] - step * (mine_ref[...] + far_ref[0:TILE, :])
    share = share0_ref[...] - step * share_ref[...]
    rays = forward_tiles(values, share, low_ref, high_ref, gamma_ref, sums_ref)
    payload_ref[...] = select_rows(one_hot(TILE, slot_ref[...]), rays)


def back_message(choice, image, rows):
    place = iota((SENT, TILE), 0) & (PAD - 1)
    head = jnp.zeros((SENT, TILE), F32)
    for where, row in rows:
        head = jnp.where(place == where, row, head)
    return select_rows(choice, image) + head


def owner_first_kernel(received_ref, gamma_ref, payload_ref, image_ref, choice_ref, compact_ref):
    received = received_ref[...]
    blocks = received.reshape(N_VOX, PAD, TILE)
    head = jnp.broadcast_to(blocks[:, MAP : MAP + 1, :], (N_VOX, PAD, TILE)).reshape(SENT, TILE)
    place, lane = iota((SENT, TILE), 0) & (PAD - 1), iota((SENT, TILE), 1)
    column = jnp.sum(jnp.where((lane == place) & (place < CAP), head, 0.0), axis=1, keepdims=True)
    hit = (column.astype(jnp.int32) == lane) & (place < CAP)
    choice = jnp.where(hit, 1.0, 0.0)
    image = select_rows(jnp.transpose(choice).astype(BF16), received)
    owned = image_ref.shape[0]
    lower = image[0:owned, :]
    image_ref[...] = lower
    square = jnp.sum(lower * lower, axis=0, keepdims=True)
    payload_ref[...] = back_message(choice.astype(BF16), image, ((NORM, square), (LOCAL, gamma_ref[0:1, :])))
    choice_ref[...] = choice
    compact_ref[...] = jnp.transpose(choice.reshape(N_VOX, PAD, TILE)[:, 0:CAP, :].reshape(TILE, TILE))


def owner_kernel(received_ref, gamma_ref, image0_ref, choice_ref, compact_ref, payload_ref, image_ref):
    image = select_rows(compact_ref[...].astype(BF16), received_ref[...])
    owned = image_ref.shape[0]
    lower = image[0:owned, :]
    image_ref[...] = lower
    square = jnp.sum(lower * lower, axis=0, keepdims=True)
    cross = jnp.sum(lower * image0_ref[...], axis=0, keepdims=True)
    rows = ((NORM, square), (LOCAL, gamma_ref[0:1, :]), (OTHER, cross))
    payload_ref[...] = back_message(choice_ref[...].astype(BF16), image, rows)


def last_kernel(
    near_ref, far_ref, inner_near_ref, inner_far_ref, scalars_ref, image0_ref, image1_ref, ray_ref,
    solution_ref, residual_ref, normal_ref,
):
    tail = near_ref[VT_DEV:SUM, :] + far_ref[VT_DEV:SUM, :]
    gamma0, square0, step0 = scalars_ref[0:1, :], scalars_ref[1:2, :], scalars_ref[2:3, :]
    gamma1 = lane_sum(tail, GAMMA)
    ratio = gamma1 / gamma0
    square1 = lane_sum(tail, IMAGE) + 2.0 * ratio * lane_sum(tail, CROSS) + ratio * ratio * square0
    step1 = gamma1 / square1
    normal0 = inner_near_ref[0:VT_DEV, :] + inner_far_ref[0:VT_DEV, :]
    change0 = inner_near_ref[VT_DEV:, :] + inner_far_ref[VT_DEV:, :]
    normal1 = normal0 - step0 * change0
    change1 = near_ref[0:VT_DEV, :] + far_ref[0:VT_DEV, :] + ratio * change0
    solution_ref[...] = step0 * normal0 + step1 * (normal1 + ratio * normal0)
    normal_ref[...] = normal1 - step1 * change1
    image0 = image0_ref[...]
    residual_ref[...] = ray_ref[...] - step0 * image0 - step1 * (image1_ref[...] + ratio * image0)


def call(kernel, outs, scratch, args, hbm=0, cost=None, limit=24):
    vmem = pl.BlockSpec(memory_space=pltpu.VMEM)
    specs = [pl.BlockSpec(memory_space=pl.ANY)] * hbm
    outs = [out if isinstance(out, jax.ShapeDtypeStruct) else jax.ShapeDtypeStruct(out, F32) for out in outs]
    return pl.pallas_call(
        kernel,
        out_shape=outs,
        in_specs=specs + [vmem] * (len(args) - hbm),
        out_specs=[vmem] * len(outs),
        scratch_shapes=[pltpu.VMEM(shape, F32) if isinstance(shape, tuple) else shape for shape in scratch],
        cost_estimate=cost,
        compiler_params=pltpu.CompilerParams(vmem_limit_bytes=limit * 1024 * 1024),
    )(*args)


def local(tile_values, tile_vox, tile_slot, slot_block, ray_data):
    owned = ray_data.shape[0]
    block = (TILE, TILE)
    sent = (SENT, TILE)
    field = (VT_DEV, TILE)
    scalar = (8, TILE)
    part = (PART, TILE)
    sums = (TILE * 8, TILE)
    rays = (owned, TILE)
    indices = jax.ShapeDtypeStruct((1, TILE), jnp.int32)

    def over_vox(array):
        return lax.all_to_all(array, "vox", 0, 0, tiled=True)

    def across(array, distance):
        return lax.ppermute(array, "row", [(index, index ^ distance) for index in range(N_ROW)])

    def quad(own):
        others = [across(own, distance) for distance in (1, 2, 3)]
        cost = pl.CostEstimate(flops=0, bytes_accessed=2**22, transcendentals=0)
        (own_field,) = call(spread_kernel, [field], [], (own,), cost=cost)
        return (own, own_field, *others)

    (copies,) = call(copies_kernel, [(CHIPS * owned, TILE)], [], (ray_data,))
    chips = [[chip * CORES + core for chip in range(CHIPS)] for core in range(CORES)]
    same = lax.all_to_all(copies, "vox", 0, 0, tiled=True, axis_index_groups=chips)
    same, tile_vox, tile_slot, slot_block = lax.optimization_barrier((same, tile_vox, tile_slot, slot_block))
    other = lax.ppermute(same, "vox", [(device, device ^ 1) for device in range(N_VOX)])
    (pack,) = call(
        pack_kernel,
        [jax.ShapeDtypeStruct(scalar, jnp.int32)],
        [],
        (tile_slot.reshape(1, TILE), slot_block, tile_vox.reshape(1, TILE)),
    )
    own, share0, natural, slot_row, slot, vox_row, extra, ids = call(
        back_first_kernel,
        [part, block, (TILE, TILE, TILE), indices, indices, indices, sent, scalar],
        [
            block,
            sums,
            pltpu.VMEM((1, TILE), jnp.int32),
            pltpu.SMEM((1, TILE), jnp.int32),
            pltpu.SemaphoreType.DMA((CHUNKS + 1,)),
        ],
        (tile_values, same, other, pack),
        hbm=1,
        limit=42,
    )
    ids = across(ids, 6)
    def relay(natural, first):
        return call(
            functools.partial(relay_kernel, first=first),
            [(HALF, TILE, TILE)],
            [],
            (natural,),
            cost=pl.CostEstimate(flops=0, bytes_accessed=2**23, transcendentals=0),
        )[0]

    messages = quad(own)
    low = relay(natural, 0)
    messages, ids, low = lax.optimization_barrier((messages, ids, low))
    near, mine, send = call(quad_first_kernel, [field, block, part], [], (*messages, ids))
    send, natural = lax.optimization_barrier((send, natural))
    far = across(send, 6)
    high = relay(natural, HALF)
    payload, values0, gamma = call(
        forward_first_kernel, [sent, block, scalar], [sums], (mine, far, share0, low, high, slot_row, extra)
    )
    payload, image0, choice, compact = call(
        owner_first_kernel, [sent, rays, sent, block], [], (over_vox(payload), gamma)
    )
    own, share = call(back_kernel, [part, block], [block], (over_vox(payload), low, high, slot_row, vox_row))
    near, mine, send = call(
        quad_kernel, [(2 * VT_DEV, TILE), block, part], [], (*quad(own), ids, near)
    )
    far, near = lax.optimization_barrier((across(send, 6), near))
    inner_far = across(near, 6)
    payload, scalars, gamma = call(
        forward_kernel,
        [block, scalar, scalar],
        [sums],
        (mine, send, far, share, values0, share0, low, high, slot),
    )
    received, inner_far = lax.optimization_barrier((over_vox(payload), inner_far))
    payload, image1 = call(owner_kernel, [sent, rays], [], (received, gamma, image0, choice, compact))
    (own,) = call(back_last_kernel, [part], [block], (over_vox(payload), low, high, slot_row, vox_row))
    (last,) = call(quad_last_kernel, [(SUM, TILE)], [], quad(own))
    return tuple(
        call(
            last_kernel,
            [field, rays, field],
            [],
            (last, across(last, 6), near, inner_far, scalars, image0, image1, ray_data),
        )
    )


def solution(mesh):
    return jax.shard_map(
        local,
        mesh=mesh,
        in_specs=(
            P(("vox", "row"), None, None),
            P(("vox", "row")),
            P(("vox", "row")),
            P(("vox", "row"), None),
            P(("vox", "row"), None),
        ),
        out_specs=(P("vox", None), P(("vox", "row"), None), P("vox", None)),
        check_vma=False,
    )
```

```python
import functools

import jax
import jax.numpy as jnp
from jax import lax
from jax.experimental import pallas as pl
from jax.experimental.pallas import tpu as pltpu
from jax.sharding import PartitionSpec as P

TILE = 128
VT_DEV = 256
CAP = 4
N_VOX = 32
N_ROW = 8
CORES = 2
HALF = TILE // 2
CHIPS = N_VOX // CORES
CHUNKS = 16
PAD = 8
MAP = CAP
NORM, LOCAL, OTHER = CAP, CAP + 1, CAP + 2
SENT = N_VOX * PAD
PART = TILE + 8
SUM = VT_DEV + 8
IDS, IMAGE, GAMMA, CROSS = 0, 1, 2, 3

F32 = jnp.float32
BF16 = jnp.bfloat16


def iota(shape, dim):
    return lax.broadcasted_iota(jnp.int32, shape, dim)


def three_terms(values):
    high = values.astype(BF16)
    rest = values - high.astype(F32)
    middle = rest.astype(BF16)
    return high, middle, (rest - middle.astype(F32)).astype(BF16)


def select_rows(choice, values):
    high, middle, low = three_terms(values)
    small = jnp.dot(choice, jnp.concatenate([middle, low], axis=1), preferred_element_type=F32)
    small = small[:, TILE:] + small[:, 0:TILE]
    return small + jnp.dot(choice, high, preferred_element_type=F32)


def select_columns(values, choice):
    rows = values.shape[0]
    terms = jnp.dot(jnp.concatenate(three_terms(values), axis=0), choice, preferred_element_type=F32)
    return (terms[2 * rows :, :] + terms[rows : 2 * rows, :]) + terms[0:rows, :]


def one_hot(rows, index):
    return jnp.where(iota((rows, TILE), 0) == index, 1.0, 0.0).astype(BF16)


def copies_kernel(ray_ref, copies_ref):
    owned = ray_ref.shape[0]
    rays = ray_ref[...]
    for chip in range(CHIPS):
        copies_ref[chip * owned : (chip + 1) * owned, :] = rays


def pack_kernel(slot_ref, map_ref, vox_ref, pack_ref):
    pack_ref[...] = jnp.zeros_like(pack_ref)
    pack_ref[0:1, :] = slot_ref[...]
    pack_ref[1:2, :] = map_ref[...]
    pack_ref[2:3, :] = vox_ref[...]


def relay_kernel(natural_ref, tiles_ref, *, first):
    def step(index, unused):
        block = natural_ref[:, pl.ds(pl.multiple_of(first + index * 8, 8), 8), :]
        block = jnp.swapaxes(block, 0, 1)
        for inner in range(8):
            tiles_ref[index * 8 + inner] = jnp.transpose(block[inner])
        return unused

    lax.fori_loop(0, HALF // 8, step, 0)


def back_tiles(low_ref, high_ref, weight_ref):
    total = jnp.zeros((TILE, TILE), F32)
    for first, tiles_ref in ((0, low_ref), (HALF, high_ref)):

        def step(index, total):
            for inner in range(8):
                ray = index * 8 + inner
                total = total + tiles_ref[ray] * weight_ref[pl.ds(first + ray, 1), :]
            return total

        total = lax.fori_loop(0, HALF // 8, step, total)
    return total


def write_tail(part_ref, vox_row, image, gamma, cross):
    sub = iota((8, TILE), 0)
    tail = jnp.where(sub == IDS, jnp.broadcast_to(vox_row.astype(F32), (8, TILE)), 0.0)
    for place, row in ((IMAGE, image), (GAMMA, gamma), (CROSS, cross)):
        if row is not None:
            tail = tail + jnp.where(sub == place, jnp.broadcast_to(row, (8, TILE)), 0.0)
    part_ref[TILE:PART, :] = tail


def back_first_kernel(
    tiles_hbm, same_ref, other_ref, pack_ref,
    part_ref, share_ref, natural_ref, row_ref, slot_ref, vox_ref, extra_ref, ids_ref,
    picked_ref, sums_ref, index_ref, place_ref, sems,
):
    size = TILE // CHUNKS
    moves = []
    for chunk in range(CHUNKS):
        where = pl.ds(chunk * size, size)
        moves.append(pltpu.make_async_copy(tiles_hbm.at[where], natural_ref.at[where], sems.at[chunk]))
    for move in moves:
        move.start()

    owned = same_ref.shape[0] // CHIPS
    slot, vox = pack_ref[0:1, :], pack_ref[2:3, :]
    target, place = lax.shift_right_logical(slot, 2), slot & (CAP - 1)
    sub, lane = iota((TILE, TILE), 0), iota((TILE, TILE), 1)
    column = jnp.transpose(jnp.broadcast_to(pack_ref[1:2, :].astype(F32), (TILE, TILE)))
    block = jnp.sum(jnp.where(sub == slot, column, 0.0), axis=0, keepdims=True).astype(jnp.int32)
    mine = lax.axis_index("vox") & (CORES - 1)
    other = (target & (CORES - 1)) ^ mine
    index_ref[...] = (other * CHIPS + lax.shift_right_logical(target, 1)) * owned + block
    move = pltpu.make_async_copy(index_ref, place_ref, sems.at[CHUNKS])
    move.start()

    row_ref[...] = target * PAD + place
    slot_ref[...] = slot
    vox_ref[...] = vox
    ids_ref[...] = jnp.broadcast_to(vox.astype(F32), (8, TILE))
    write_tail(part_ref, vox, None, None, None)
    values = jnp.where((sub & (CAP - 1)) == lane, column, 0.0).astype(BF16)
    sub, lane = iota((SENT, TILE), 0), iota((SENT, TILE), 1)
    hit = ((sub & (PAD - 1)) == MAP) & (lax.shift_right_logical(lane, 2) == lax.shift_right_logical(sub, 3))
    choice = jnp.where(hit, 1.0, 0.0).astype(BF16)
    extra_ref[...] = jnp.dot(choice, values, preferred_element_type=F32)

    move.wait()
    half = same_ref.shape[0]
    for tile in range(TILE):
        index = place_ref[0, tile]
        here = index < half
        row = index & (half - 1)
        picked_ref[tile : tile + 1, :] = jnp.where(here, same_ref[pl.ds(row, 1), :], other_ref[pl.ds(row, 1), :])
    weight = jnp.transpose(picked_ref[...])
    for group in range(TILE // 8):
        if group * 8 % size == 0:
            moves[group * 8 // size].wait()
        for tile in range(group * 8, group * 8 + 8):
            product = natural_ref[tile] * weight[:, tile : tile + 1]
            sums_ref[tile * 8 : tile * 8 + 8, :] = jnp.sum(product.reshape(TILE // 8, 8, TILE), axis=0)
    share = sums_ref[pl.ds(0, TILE, stride=8), :]
    for inner in range(1, 8):
        share = share + sums_ref[pl.ds(inner, TILE, stride=8), :]
    part_ref[0:TILE, :] = share
    share_ref[...] = jnp.transpose(share)


def back_share(received_ref, low_ref, high_ref, row_ref, vox_ref, part_ref, weight_ref):
    received = received_ref[...]
    weight_ref[...] = select_columns(jnp.transpose(received), one_hot(SENT, row_ref[...]))
    heads = jnp.sum(received.reshape(N_VOX, PAD, TILE), axis=0)
    share = back_tiles(low_ref, high_ref, weight_ref)
    part_ref[0:TILE, :] = jnp.transpose(share)
    write_tail(part_ref, vox_ref[...], *(heads[row : row + 1, :] for row in (NORM, LOCAL, OTHER)))
    return share


def back_kernel(received_ref, low_ref, high_ref, row_ref, vox_ref, part_ref, share_ref, weight_ref):
    share_ref[...] = back_share(received_ref, low_ref, high_ref, row_ref, vox_ref, part_ref, weight_ref)


def back_last_kernel(received_ref, low_ref, high_ref, row_ref, vox_ref, part_ref, weight_ref):
    back_share(received_ref, low_ref, high_ref, row_ref, vox_ref, part_ref, weight_ref)


def spread(ref):
    where = ref[TILE + IDS : TILE + IDS + 1, :].astype(jnp.int32)
    return select_rows(one_hot(VT_DEV, where), ref[0:TILE, :])


def spread_kernel(own_ref, spread_ref):
    spread_ref[...] = spread(own_ref)


def quad_sum(own_ref, spread_ref, one_ref, two_ref, three_ref):
    field = (spread_ref[...] + spread(one_ref)) + (spread(two_ref) + spread(three_ref))
    tail = slice(TILE, PART)
    return field, (own_ref[tail, :] + one_ref[tail, :]) + (two_ref[tail, :] + three_ref[tail, :])


def read_tiles(field, tail, own_ref, ids_ref, mine_ref, send_ref):
    here = one_hot(VT_DEV, own_ref[TILE + IDS : TILE + IDS + 1, :].astype(jnp.int32))
    there = one_hot(VT_DEV, ids_ref[0:1, :].astype(jnp.int32))
    both = select_columns(jnp.transpose(field), jnp.concatenate([here, there], axis=1))
    mine_ref[...] = both[:, 0:TILE]
    send_ref[0:TILE, :] = both[:, TILE : 2 * TILE]
    send_ref[TILE:PART, :] = tail


def quad_first_kernel(own_ref, spread_ref, one_ref, two_ref, three_ref, ids_ref, near_ref, mine_ref, send_ref):
    field, tail = quad_sum(own_ref, spread_ref, one_ref, two_ref, three_ref)
    read_tiles(field, tail, own_ref, ids_ref, mine_ref, send_ref)
    near_ref[...] = field


def quad_kernel(own_ref, spread_ref, one_ref, two_ref, three_ref, ids_ref, before_ref, near_ref, mine_ref, send_ref):
    field, tail = quad_sum(own_ref, spread_ref, one_ref, two_ref, three_ref)
    read_tiles(field, tail, own_ref, ids_ref, mine_ref, send_ref)
    near_ref[0:VT_DEV, :] = before_ref[...]
    near_ref[VT_DEV:, :] = field


def quad_last_kernel(own_ref, spread_ref, one_ref, two_ref, three_ref, near_ref):
    field, tail = quad_sum(own_ref, spread_ref, one_ref, two_ref, three_ref)
    near_ref[0:VT_DEV, :] = field
    near_ref[VT_DEV:SUM, :] = tail


def forward_tiles(values, share, low_ref, high_ref, gamma_ref, sums_ref):
    for first, tiles_ref in ((0, low_ref), (HALF, high_ref)):

        def step(index, unused):
            for inner in range(8):
                ray = index * 8 + inner
                product = tiles_ref[ray] * values
                row = pl.multiple_of((first + ray) * 8, 8)
                sums_ref[pl.ds(row, 8), :] = jnp.sum(product.reshape(TILE // 8, 8, TILE), axis=0)
            return unused

        lax.fori_loop(0, HALF // 8, step, 0)
    gamma_ref[...] = jnp.broadcast_to(jnp.sum(values * share, axis=0, keepdims=True), (8, TILE))
    rays = sums_ref[pl.ds(0, TILE, stride=8), :]
    for inner in range(1, 8):
        rays = rays + sums_ref[pl.ds(inner, TILE, stride=8), :]
    return jnp.transpose(rays)


def forward_first_kernel(
    mine_ref, far_ref, share_ref, low_ref, high_ref, row_ref, extra_ref, payload_ref, values_ref, gamma_ref, sums_ref
):
    values = mine_ref[...] + far_ref[0:TILE, :]
    values_ref[...] = values
    rays = forward_tiles(values, share_ref[...], low_ref, high_ref, gamma_ref, sums_ref)
    payload_ref[...] = select_rows(one_hot(SENT, row_ref[...]), rays) + extra_ref[...]


def lane_sum(tail, place):
    return jnp.sum(tail[place : place + 1, :], axis=1, keepdims=True)


def forward_kernel(
    mine_ref, send_ref, far_ref, share_ref, values0_ref, share0_ref, low_ref, high_ref, slot_ref,
    payload_ref, scalars_ref, gamma_ref, sums_ref,
):
    tail = send_ref[TILE:PART, :] + far_ref[TILE:PART, :]
    gamma, square = lane_sum(tail, GAMMA), lane_sum(tail, IMAGE)
    step = gamma / square
    sub = iota((8, TILE), 0)
    scalars_ref[...] = jnp.where(sub == 0, gamma, jnp.where(sub == 1, square, step))
    values = values0_ref[...] - step * (mine_ref[...] + far_ref[0:TILE, :])
    share = share0_ref[...] - step * share_ref[...]
    rays = forward_tiles(values, share, low_ref, high_ref, gamma_ref, sums_ref)
    payload_ref[...] = select_rows(one_hot(TILE, slot_ref[...]), rays)


def back_message(choice, image, rows):
    place = iota((SENT, TILE), 0) & (PAD - 1)
    head = jnp.zeros((SENT, TILE), F32)
    for where, row in rows:
        head = jnp.where(place == where, row, head)
    return select_rows(choice, image) + head


def owner_first_kernel(received_ref, gamma_ref, payload_ref, image_ref, choice_ref, compact_ref):
    received = received_ref[...]
    blocks = received.reshape(N_VOX, PAD, TILE)
    head = jnp.broadcast_to(blocks[:, MAP : MAP + 1, :], (N_VOX, PAD, TILE)).reshape(SENT, TILE)
    place, lane = iota((SENT, TILE), 0) & (PAD - 1), iota((SENT, TILE), 1)
    column = jnp.sum(jnp.where((lane == place) & (place < CAP), head, 0.0), axis=1, keepdims=True)
    hit = (column.astype(jnp.int32) == lane) & (place < CAP)
    choice = jnp.where(hit, 1.0, 0.0)
    image = select_rows(jnp.transpose(choice).astype(BF16), received)
    owned = image_ref.shape[0]
    lower = image[0:owned, :]
    image_ref[...] = lower
    square = jnp.sum(lower * lower, axis=0, keepdims=True)
    payload_ref[...] = back_message(choice.astype(BF16), image, ((NORM, square), (LOCAL, gamma_ref[0:1, :])))
    choice_ref[...] = choice
    compact_ref[...] = jnp.transpose(choice.reshape(N_VOX, PAD, TILE)[:, 0:CAP, :].reshape(TILE, TILE))


def owner_kernel(received_ref, gamma_ref, image0_ref, choice_ref, compact_ref, payload_ref, image_ref):
    image = select_rows(compact_ref[...].astype(BF16), received_ref[...])
    owned = image_ref.shape[0]
    lower = image[0:owned, :]
    image_ref[...] = lower
    square = jnp.sum(lower * lower, axis=0, keepdims=True)
    cross = jnp.sum(lower * image0_ref[...], axis=0, keepdims=True)
    rows = ((NORM, square), (LOCAL, gamma_ref[0:1, :]), (OTHER, cross))
    payload_ref[...] = back_message(choice_ref[...].astype(BF16), image, rows)


def last_kernel(
    near_ref, far_ref, inner_near_ref, inner_far_ref, scalars_ref, image0_ref, image1_ref, ray_ref,
    solution_ref, residual_ref, normal_ref,
):
    tail = near_ref[VT_DEV:SUM, :] + far_ref[VT_DEV:SUM, :]
    gamma0, square0, step0 = scalars_ref[0:1, :], scalars_ref[1:2, :], scalars_ref[2:3, :]
    gamma1 = lane_sum(tail, GAMMA)
    ratio = gamma1 / gamma0
    square1 = lane_sum(tail, IMAGE) + 2.0 * ratio * lane_sum(tail, CROSS) + ratio * ratio * square0
    step1 = gamma1 / square1
    normal0 = inner_near_ref[0:VT_DEV, :] + inner_far_ref[0:VT_DEV, :]
    change0 = inner_near_ref[VT_DEV:, :] + inner_far_ref[VT_DEV:, :]
    normal1 = normal0 - step0 * change0
    change1 = near_ref[0:VT_DEV, :] + far_ref[0:VT_DEV, :] + ratio * change0
    solution_ref[...] = step0 * normal0 + step1 * (normal1 + ratio * normal0)
    normal_ref[...] = normal1 - step1 * change1
    image0 = image0_ref[...]
    residual_ref[...] = ray_ref[...] - step0 * image0 - step1 * (image1_ref[...] + ratio * image0)


def call(kernel, outs, scratch, args, hbm=0, cost=None, limit=24):
    vmem = pl.BlockSpec(memory_space=pltpu.VMEM)
    specs = [pl.BlockSpec(memory_space=pl.ANY)] * hbm
    outs = [out if isinstance(out, jax.ShapeDtypeStruct) else jax.ShapeDtypeStruct(out, F32) for out in outs]
    return pl.pallas_call(
        kernel,
        out_shape=outs,
        in_specs=specs + [vmem] * (len(args) - hbm),
        out_specs=[vmem] * len(outs),
        scratch_shapes=[pltpu.VMEM(shape, F32) if isinstance(shape, tuple) else shape for shape in scratch],
        cost_estimate=cost,
        compiler_params=pltpu.CompilerParams(vmem_limit_bytes=limit * 1024 * 1024),
    )(*args)


def local(tile_values, tile_vox, tile_slot, slot_block, ray_data):
    owned = ray_data.shape[0]
    block = (TILE, TILE)
    sent = (SENT, TILE)
    field = (VT_DEV, TILE)
    scalar = (8, TILE)
    part = (PART, TILE)
    sums = (TILE * 8, TILE)
    rays = (owned, TILE)
    indices = jax.ShapeDtypeStruct((1, TILE), jnp.int32)

    def over_vox(array):
        return lax.all_to_all(array, "vox", 0, 0, tiled=True)

    def across(array, distance):
        return lax.ppermute(array, "row", [(index, index ^ distance) for index in range(N_ROW)])

    def quad(own):
        others = [across(own, distance) for distance in (1, 2, 3)]
        cost = pl.CostEstimate(flops=0, bytes_accessed=2**22, transcendentals=0)
        (own_field,) = call(spread_kernel, [field], [], (own,), cost=cost)
        return (own, own_field, *others)

    (copies,) = call(copies_kernel, [(CHIPS * owned, TILE)], [], (ray_data,))
    chips = [[chip * CORES + core for chip in range(CHIPS)] for core in range(CORES)]
    same = lax.all_to_all(copies, "vox", 0, 0, tiled=True, axis_index_groups=chips)
    same, tile_vox, tile_slot, slot_block = lax.optimization_barrier((same, tile_vox, tile_slot, slot_block))
    other = lax.ppermute(same, "vox", [(device, device ^ 1) for device in range(N_VOX)])
    (pack,) = call(
        pack_kernel,
        [jax.ShapeDtypeStruct(scalar, jnp.int32)],
        [],
        (tile_slot.reshape(1, TILE), slot_block, tile_vox.reshape(1, TILE)),
    )
    own, share0, natural, slot_row, slot, vox_row, extra, ids = call(
        back_first_kernel,
        [part, block, (TILE, TILE, TILE), indices, indices, indices, sent, scalar],
        [
            block,
            sums,
            pltpu.VMEM((1, TILE), jnp.int32),
            pltpu.SMEM((1, TILE), jnp.int32),
            pltpu.SemaphoreType.DMA((CHUNKS + 1,)),
        ],
        (tile_values, same, other, pack),
        hbm=1,
        limit=42,
    )
    ids = across(ids, 6)
    def relay(natural, first):
        return call(
            functools.partial(relay_kernel, first=first),
            [(HALF, TILE, TILE)],
            [],
            (natural,),
            cost=pl.CostEstimate(flops=0, bytes_accessed=2**23, transcendentals=0),
        )[0]

    messages = quad(own)
    low = relay(natural, 0)
    messages, ids, low = lax.optimization_barrier((messages, ids, low))
    near, mine, send = call(quad_first_kernel, [field, block, part], [], (*messages, ids))
    send, natural = lax.optimization_barrier((send, natural))
    far = across(send, 6)
    high = relay(natural, HALF)
    payload, values0, gamma = call(
        forward_first_kernel, [sent, block, scalar], [sums], (mine, far, share0, low, high, slot_row, extra)
    )
    payload, image0, choice, compact = call(
        owner_first_kernel, [sent, rays, sent, block], [], (over_vox(payload), gamma)
    )
    own, share = call(back_kernel, [part, block], [block], (over_vox(payload), low, high, slot_row, vox_row))
    near, mine, send = call(
        quad_kernel, [(2 * VT_DEV, TILE), block, part], [], (*quad(own), ids, near)
    )
    far, near = lax.optimization_barrier((across(send, 6), near))
    inner_far = across(near, 6)
    payload, scalars, gamma = call(
        forward_kernel,
        [block, scalar, scalar],
        [sums],
        (mine, send, far, share, values0, share0, low, high, slot),
    )
    received, inner_far = lax.optimization_barrier((over_vox(payload), inner_far))
    payload, image1 = call(owner_kernel, [sent, rays], [], (received, gamma, image0, choice, compact))
    (own,) = call(back_last_kernel, [part], [block], (over_vox(payload), low, high, slot_row, vox_row))
    (last,) = call(quad_last_kernel, [(SUM, TILE)], [], quad(own))
    return tuple(
        call(
            last_kernel,
            [field, rays, field],
            [],
            (last, across(last, 6), near, inner_far, scalars, image0, image1, ray_data),
        )
    )


def solution(mesh):
    return jax.shard_map(
        local,
        mesh=mesh,
        in_specs=(
            P(("vox", "row"), None, None),
            P(("vox", "row")),
            P(("vox", "row")),
            P(("vox", "row"), None),
            P(("vox", "row"), None),
        ),
        out_specs=(P("vox", None), P(("vox", "row"), None), P("vox", None)),
        check_vma=False,
    )
```
